32 devices in a mesh: groups: 2 (over y), adapter: 4 (over z), tensor: 4 (over x, core).
Axes of the slice: x: 2, y: 2, z: 4, core: 2. Of those that a mesh axis runs over, the one named last changes fastest.
Arguments:
- hidden: bfloat16 [256, 8192], P(('groups', 'adapter'), 'tensor'), parts along dimension 0, may hold values from -6 to 6
- base_queries: bfloat16 [256, 8192], P(('groups', 'adapter'), 'tensor'), parts along dimension 0, may hold values from -6 to 6
- base_keys: bfloat16 [256, 1024], P(('groups', 'adapter'), 'tensor'), parts along dimension 0, may hold values from -6 to 6
- base_values: bfloat16 [256, 1024], P(('groups', 'adapter'), 'tensor'), parts along dimension 0, may hold values from -6 to 6
- adapter_down_weight: bfloat16 [32, 96, 8192], P('adapter', None, 'tensor'), may hold values from -0.0625 to 0.0625
- adapter_up_query: bfloat16 [32, 32, 8192], P(None, None, ('adapter', 'tensor')), may hold values from -1 to 1
- adapter_up_key_value: bfloat16 [32, 2, 32, 1024], P(None, None, None, ('adapter', 'tensor')), may hold values from -1 to 1
- cached_keys: bfloat16 [256, 8, 128, 128], P(('groups', 'adapter'), 'tensor'), parts along dimension 0, may hold values from -400 to 400
- cached_values: bfloat16 [256, 8, 128, 128], P(('groups', 'adapter'), 'tensor'), parts along dimension 0, may hold values from -6 to 6
- request_adapter: int32 [256], P(('groups', 'adapter')), parts along dimension 0, may hold values from 0 to 31
- lengths: int32 [256], P(('groups', 'adapter')), parts along dimension 0, may hold values from 1 to 128, 8192 in all
Outputs:
- attention: bfloat16 [256, 8192], P(('groups', 'adapter'), 'tensor'), parts along dimension 0
- fresh_keys: bfloat16 [256, 1024], P(('groups', 'adapter'), 'tensor'), parts along dimension 0
- fresh_values: bfloat16 [256, 1024], P(('groups', 'adapter'), 'tensor'), parts along dimension 0
The draws below stay inside these ranges and needn't reach their ends.
There are 2 independent parts, one for each index of `groups`. The reference program is written for one: setup_inputs(seed, part) draws one part's arguments, and reference() takes and returns one part's arrays. A program takes and returns all parts, laid end to end along the dimension named above; an argument that names none is the same for every part. Nothing has to cross between parts.
Inputs may be any that keep to these rules, and one draw needn't show every extreme that they name: The lengths of the 128 requests of ONE part (one serving replica) sum to 8192, and some request of each part has exactly 128; over an array that lays several parts end to end the total is that sum times the number of parts.
All inputs are finite; a program needn't handle non-finite values. No bound on the sum of `lengths` on one device may be relied on, other than what follows from the above.
Results may differ from the reference program's by a relative error of at most 0.0088.
Values may be sent and summed in bfloat16 or wider, within the bound.
No kernel may reach another device: no remote copies, remote signals or barrier semaphores. Data moves between devices by JAX's collectives and lax.ppermute only.
A program may use at most 64 MiB of HBM per device.

```python
import math
import jax
import jax.numpy as jnp
import numpy as np
from jax import lax

MODEL_WIDTH = 8192
QUERY_HEAD_COUNT = 64
KEY_VALUE_HEADS = 8
HEAD_SIZE = 128
ADAPTER_RANK = 32
CACHE_SLOTS = 128
ADAPTER_COUNT = 32
REQUEST_COUNT = 128


def draw_cached_keys(key, part):
    key = jax.random.fold_in(key, 11)
    key_drawn = jax.random.fold_in(key, 0)
    array_shape = (REQUEST_COUNT, KEY_VALUE_HEADS, CACHE_SLOTS, HEAD_SIZE)
    drawn_keys = jnp.clip(jax.random.normal(key_drawn, array_shape, jnp.float32), -4.0, 4.0)
    return drawn_keys.astype(jnp.bfloat16)


def plant(array, own_key, smallest, high):
    shape = array.shape
    index_at = [jax.random.randint(jax.random.fold_in(own_key, axis), (), 0, shape[axis]) for axis in range(len(shape))]
    array = array.at[tuple(index_at)].set(smallest)
    longest = shape.index(max(shape))
    index_at[longest] = (index_at[longest] + 1) % shape[longest]
    return array.at[tuple(index_at)].set(high)


def levels(rng, dims, cuts, low, top_value):
    def one(position, parts):
        steps = jax.random.uniform(jax.random.fold_in(jax.random.fold_in(rng, 6), position), (parts,), jnp.float32, low / len(cuts), top_value / len(cuts))
        return jnp.repeat(jnp.exp(steps), dims[position] // parts).reshape((-1,) + (1,) * (len(dims) - position - 1))

    factor_of = one(*cuts[0])
    for cut in cuts[1:]:
        factor_of = factor_of * one(*cut)
    return factor_of


def rank_table(count, slope):
    portions = [(1 << 20) // math.isqrt(grade ** slope) + 1 for grade in range(1, count + 1)]
    deviation = 1 + sum(portions) // (1 << 30)
    return np.cumsum(np.array([max(1, weight // deviation) for weight in portions]))


def ranked(stream_key, extent, count, skew):
    table = rank_table(count, skew)
    lot = jax.random.randint(jax.random.fold_in(stream_key, 1), extent, 0, int(table[count - 1]))
    grade = jnp.searchsorted(jnp.asarray(table, jnp.int32), lot, side="right")
    return jax.random.permutation(jax.random.fold_in(stream_key, 2), count)[grade].astype(jnp.int32)


def length_profile(count, total, bound, skew):
    loads = [(1 << 20) // math.isqrt(standing ** skew) + 1 for standing in range(2, count + 1)]
    spare, counts = total - bound - (count - 1), [1] * (count - 1)
    while spare > 0:
        movable = [i for i in range(count - 1) if counts[i] < bound]
        whole, budget = sum([loads[i] for i in movable]), spare
        for i in movable:
            addition = min(bound - counts[i], max(1, budget * loads[i] // whole), spare)
            counts[i] = counts[i] + addition
            spare = spare - addition
    return np.array([bound] + counts)


def ragged_sizes(stream_key, amount, total, limit, slope):
    if amount == 2:
        one = jax.random.randint(stream_key, (), max(1, total - limit), min(limit, total - 1) + 1)
        return jnp.stack([one, total - one])
    sizes = jnp.asarray(length_profile(amount, total, limit, slope), jnp.int32)
    couples = (amount - 1) // 2
    giver, sink = sizes[1:1 + 2 * couples:2], sizes[2:2 + 2 * couples:2]
    slack = jnp.minimum(giver - 1, limit - sink)
    passed = jax.random.randint(jax.random.fold_in(stream_key, 1), (couples,), 0, 1 << 20) % (slack + 1)
    sizes = sizes.at[1:1 + 2 * couples:2].set(giver - passed).at[2:2 + 2 * couples:2].set(sink + passed)
    return sizes[jax.random.permutation(jax.random.fold_in(stream_key, 2), amount)]


def bell_draw(own_key, extent, width, most, cuts=(), held_as=jnp.bfloat16):
    drawn = width * jax.random.normal(own_key, extent, jnp.float32)
    if cuts:
        drawn = drawn * levels(own_key, extent, cuts, -0.22, 0.18)
    return jnp.clip(drawn, -most, most).astype(held_as)


def setup_inputs(seed: int = 0, part: int = 0) -> dict:
    keys = jax.random.split(jax.random.key(seed), 12)
    part_splits = jax.random.split(jax.random.fold_in(keys[11], part), 12)
    return {
        "hidden": bell_draw(part_splits[0], (REQUEST_COUNT, MODEL_WIDTH), 1.0, 6.0, ((0, 4), (1, 4))),
        "base_queries": bell_draw(part_splits[1], (REQUEST_COUNT, QUERY_HEAD_COUNT * HEAD_SIZE), 1.0, 6.0, ((0, 4), (1, 4))),
        "base_keys": bell_draw(part_splits[2], (REQUEST_COUNT, KEY_VALUE_HEADS * HEAD_SIZE), 1.0, 6.0, ((0, 4), (1, 4))),
        "base_values": bell_draw(part_splits[3], (REQUEST_COUNT, KEY_VALUE_HEADS * HEAD_SIZE), 1.0, 6.0, ((0, 4), (1, 4))),
        "adapter_down_weight": bell_draw(keys[4], (ADAPTER_COUNT, 3 * ADAPTER_RANK, MODEL_WIDTH), MODEL_WIDTH ** -0.5, 0.0625, ((0, 4), (2, 4))),
        "adapter_up_query": bell_draw(keys[5], (ADAPTER_COUNT, ADAPTER_RANK, QUERY_HEAD_COUNT * HEAD_SIZE), ADAPTER_RANK ** -0.5, 1.0, ((2, 16),)),
        "adapter_up_key_value": bell_draw(keys[6], (ADAPTER_COUNT, 2, ADAPTER_RANK, KEY_VALUE_HEADS * HEAD_SIZE), ADAPTER_RANK ** -0.5, 1.0, ((3, 16),)),
        "cached_keys": draw_cached_keys(jax.random.fold_in(jax.random.fold_in(keys[11], part), 71), part),
        "cached_values": bell_draw(part_splits[8], (REQUEST_COUNT, KEY_VALUE_HEADS, CACHE_SLOTS, HEAD_SIZE), 1.0, 6.0, ((0, 4), (1, 4))),
        "request_adapter": plant(ranked(part_splits[9], (REQUEST_COUNT,), ADAPTER_COUNT, 2), jax.random.fold_in(part_splits[9], 3), 0, ADAPTER_COUNT - 1).astype(jnp.int32),
        "lengths": ragged_sizes(part_splits[10], REQUEST_COUNT, REQUEST_COUNT * CACHE_SLOTS // 2, CACHE_SLOTS, 2).astype(jnp.int32),
    }


ADAPTER_SCALE = 0.5
ROPE_BASE = 500000.0

def rotate_pairs(vectors, positions):
    half_dim = vectors.shape[-1] // 2
    inv_freq = jnp.exp(-jnp.arange(half_dim, dtype=jnp.float32) * (2.0 / vectors.shape[-1]) * math.log(ROPE_BASE))
    angles = positions.astype(jnp.float32)[:, None, None] * inv_freq[None, None, :]
    cosine = jnp.cos(angles)
    sine_part = jnp.sin(angles)
    front_half = vectors[..., :half_dim]
    back_half = vectors[..., half_dim:]
    return jnp.concatenate([front_half * cosine - back_half * sine_part, front_half * sine_part + back_half * cosine], axis=-1)

def attend_cache(query_vector, key_new, value_new, cached_keys, cached_values, lengths):
    local_requests, query_heads, head_dim = query_vector.shape
    kv_heads = key_new.shape[1]
    grouped = query_vector.reshape(local_requests, kv_heads, query_heads // kv_heads, head_dim).astype(jnp.float32)
    inv_sqrt = 1.0 / math.sqrt(head_dim)
    cache_scores = jnp.einsum('rkge,rkpe->rkgp', grouped, cached_keys.astype(jnp.float32)) * inv_sqrt
    in_cache = jnp.arange(cached_keys.shape[2], dtype=jnp.int32)[None, :] < lengths[:, None]
    cache_scores = jnp.where(in_cache[:, None, None, :], cache_scores, -jnp.inf)
    new_score = jnp.einsum('rkge,rke->rkg', grouped, key_new.astype(jnp.float32)) * inv_sqrt
    row_max = jnp.maximum(lax.optimization_barrier(jnp.max(cache_scores, axis=-1)), new_score)
    cache_weights = jnp.exp(cache_scores - row_max[..., None])
    new_weight = jnp.exp(new_score - row_max)
    softmax_sum = lax.optimization_barrier(jnp.sum(cache_weights, axis=-1)) + new_weight
    cache_weights = (cache_weights / softmax_sum[..., None]).astype(jnp.bfloat16)
    new_weight = (new_weight / softmax_sum).astype(jnp.bfloat16)
    mixed = jnp.einsum('rkgp,rkpe->rkge', cache_weights.astype(jnp.float32), cached_values.astype(jnp.float32))
    mixed = mixed + new_weight.astype(jnp.float32)[..., None] * value_new.astype(jnp.float32)[:, :, None, :]
    return mixed.reshape(local_requests, query_heads * head_dim).astype(jnp.bfloat16)

def reference(hidden, base_queries, base_keys, base_values, adapter_down_weight, adapter_up_query, adapter_up_key_value, cached_keys, cached_values, request_adapter, lengths):

    def one_request(pair_in):
        hidden_row, adapter_slot = pair_in
        lowered_rows = lax.dynamic_index_in_dim(adapter_down_weight, adapter_slot, 0, keepdims=False)
        shrink_rank = jnp.dot(lowered_rows, hidden_row, preferred_element_type=jnp.float32).astype(jnp.bfloat16)
        raised_query = lax.dynamic_index_in_dim(adapter_up_query, adapter_slot, 0, keepdims=False)
        up_key_value = lax.dynamic_index_in_dim(adapter_up_key_value, adapter_slot, 0, keepdims=False)
        query_update = ADAPTER_SCALE * jnp.dot(shrink_rank[:ADAPTER_RANK], raised_query, preferred_element_type=jnp.float32)
        key_update = ADAPTER_SCALE * jnp.dot(shrink_rank[ADAPTER_RANK:2 * ADAPTER_RANK], up_key_value[0], preferred_element_type=jnp.float32)
        value_update = ADAPTER_SCALE * jnp.dot(shrink_rank[2 * ADAPTER_RANK:], up_key_value[1], preferred_element_type=jnp.float32)
        return (query_update, key_update, value_update)
    query_update, key_update, value_update = lax.map(one_request, (hidden, request_adapter))
    local_requests = hidden.shape[0]
    query_vector = rotate_pairs((base_queries.astype(jnp.float32) + query_update).reshape(local_requests, QUERY_HEAD_COUNT, HEAD_SIZE), lengths).astype(jnp.bfloat16)
    fresh_keys = rotate_pairs((base_keys.astype(jnp.float32) + key_update).reshape(local_requests, KEY_VALUE_HEADS, HEAD_SIZE), lengths).astype(jnp.bfloat16)
    fresh_values = (base_values.astype(jnp.float32) + value_update).astype(jnp.bfloat16)
    attention = attend_cache(query_vector, fresh_keys, fresh_values.reshape(local_requests, KEY_VALUE_HEADS, HEAD_SIZE), cached_keys, cached_values, lengths)
    return (attention, fresh_keys.reshape(local_requests, KEY_VALUE_HEADS * HEAD_SIZE), fresh_values)
```

```python
import functools
import math

import jax
import jax.numpy as jnp
from jax import lax
from jax.experimental import pallas as pl
from jax.experimental.pallas import tpu as pltpu
from jax.sharding import PartitionSpec as P

ADAPTER_SCALE = 0.5
ROPE_BASE = 500000.0
LANES = 128
VMEM_BYTES = 16 * 1024 * 1024


def rotation_factors(positions, head_dim):
    half_dim = head_dim // 2
    inv_freq = jnp.exp(
        -jnp.arange(half_dim, dtype=jnp.float32) * (2.0 / head_dim) * math.log(ROPE_BASE)
    )
    angles = positions.astype(jnp.float32)[:, None] * inv_freq[None, :]
    return jnp.cos(angles), jnp.sin(angles)


def swap_blocks(row, place, block):
    lane = lax.broadcasted_iota(jnp.int32, row.shape, 1)
    far = pltpu.roll(row, 2 * block, 1)
    row = jnp.where((place & 2) != 0, far, row)
    up, down = pltpu.roll(row, block, 1), pltpu.roll(row, LANES - block, 1)
    near = jnp.where((lane // block) % 2 == 0, down, up)
    return jnp.where((place & 1) != 0, near, row)


def down_kernel(place_ref, ids_ref, *refs):
    *hidden_refs, down_ref, out_ref, ids_out_ref, rows_ref = refs
    place = place_ref[0]
    block = hidden_refs[0].shape[0]
    for k, hidden_ref in enumerate(hidden_refs):
        start = pl.multiple_of((place ^ k) * block, block)
        rows_ref[pl.ds(start, block), :] = hidden_ref[...]
    held = down_ref.shape[0]
    ids = swap_blocks(jnp.broadcast_to(ids_ref[...], (8, LANES)), place, block)[0:1]
    ids_out_ref[...] = ids
    product = lax.dot_general(
        down_ref[...].reshape(held * down_ref.shape[1], down_ref.shape[2]),
        rows_ref[...],
        (((1,), (1,)), ((), ())),
        preferred_element_type=jnp.float32,
    )
    slot = ids - place * held
    rank = down_ref.shape[1]
    total = jnp.zeros(out_ref.shape, jnp.float32)
    for s in range(held):
        total += jnp.where(slot == s, product[s * rank : (s + 1) * rank], 0.0)
    out_ref[...] = total


def up_kernel(place_ref, ids_ref, *refs):
    shrink_refs = refs[:4]
    up_query_ref, up_kv_ref, *out_refs, terms_ref = refs[4:]
    shrink = shrink_refs[0][...].astype(jnp.float32)
    for ref in shrink_refs[1:]:
        shrink += ref[...].astype(jnp.float32)
    rank = shrink.shape[0] // 3
    rows = shrink.shape[1]
    shrink = jnp.concatenate([shrink, jnp.zeros((LANES - 3 * rank, rows), jnp.float32)], axis=0)
    shrink = jnp.transpose(shrink)
    ids = jnp.transpose(jnp.broadcast_to(ids_ref[...].astype(jnp.float32), (LANES, rows)))
    lane = lax.broadcasted_iota(jnp.int32, (rows, LANES), 1)
    count = up_query_ref.shape[0]
    query = jnp.concatenate([shrink[:, :rank]] * (LANES // rank), axis=1)
    lane_slot = (lane // rank).astype(jnp.float32)
    step = LANES // rank
    spread = jnp.concatenate(
        [
            jnp.where(ids - c * step == lane_slot, query, 0.0).astype(jnp.bfloat16)
            for c in range(count // step)
        ],
        axis=1,
    )
    terms_ref[:, : up_query_ref.shape[2]] = ADAPTER_SCALE * jnp.dot(
        spread,
        up_query_ref[...].reshape(count * rank, up_query_ref.shape[2]),
        preferred_element_type=jnp.float32,
    )
    pair = jnp.concatenate([shrink[:, rank : 3 * rank]] * (LANES // (2 * rank)), axis=1)
    lane_slot = (lane // (2 * rank)).astype(jnp.float32)
    is_key = (lane // rank) % 2 == 0
    key, value = jnp.where(is_key, pair, 0.0), jnp.where(is_key, 0.0, pair)
    step = LANES // (2 * rank)
    both = []
    for part in (key, value):
        both.append(
            jnp.concatenate(
                [
                    jnp.where(ids - c * step == lane_slot, part, 0.0).astype(jnp.bfloat16)
                    for c in range(count // step)
                ],
                axis=1,
            )
        )
    kv_width = up_kv_ref.shape[3]
    kv = ADAPTER_SCALE * jnp.dot(
        jnp.concatenate(both, axis=0),
        up_kv_ref[...].reshape(count * 2 * rank, kv_width),
        preferred_element_type=jnp.float32,
    )
    terms_ref[:, up_query_ref.shape[2] :] = jnp.concatenate([kv[:rows], kv[rows:]], axis=1)
    block = out_refs[0].shape[0]
    for k, out_ref in enumerate(out_refs):
        start = pl.multiple_of((place_ref[1] ^ k) * block, block)
        out_ref[...] = terms_ref[pl.ds(start, block), :]


def attend_kernel(place_ref, lengths_ref, *refs):
    term_refs = refs[:4]
    (
        base_query_ref,
        base_key_ref,
        base_value_ref,
        cosine_ref,
        sine_ref,
        keys_ref,
        values_ref,
        out_ref,
        fresh_key_ref,
        fresh_value_ref,
        terms_ref,
        query_ref,
        key_ref,
        value_ref,
        score_ref,
        weight_ref,
        new_weight_ref,
    ) = refs[4:]
    place = place_ref[0]
    for k, term_ref in enumerate(term_refs):
        terms_ref[place ^ k] = term_ref[...]
    requests = base_query_ref.shape[0]
    kv_heads = keys_ref.shape[1]
    slots, head = keys_ref.shape[2], keys_ref.shape[3]
    half = head // 2
    heads = base_query_ref.shape[1] // head
    group = heads // kv_heads
    each = terms_ref.shape[2] // head - 1
    cosine, sine = cosine_ref[...], sine_ref[...]
    lane = lax.broadcasted_iota(jnp.int32, (requests, head), 1)
    cosine = jnp.concatenate([cosine, cosine], axis=1)
    sine = jnp.concatenate([-sine, sine], axis=1)

    def rotate(u):
        return (u * cosine + pltpu.roll(u, half, 1) * sine).astype(jnp.bfloat16)

    for h in range(heads):
        c = (h % each) * head
        u = base_query_ref[:, h * head : (h + 1) * head].astype(jnp.float32)
        u += terms_ref[h // each, :, c : c + head]
        query_ref[pl.ds(h, requests, stride=heads), :] = rotate(u).astype(jnp.float32)
    for g in range(kv_heads):
        low = terms_ref[2 * g, :, each * head :]
        high = terms_ref[2 * g + 1, :, each * head :]
        u = base_key_ref[:, g * head : (g + 1) * head].astype(jnp.float32)
        u += jnp.where(lane < half, low, pltpu.roll(high, half, 1))
        key = rotate(u)
        fresh_key_ref[:, g * head : (g + 1) * head] = key
        key_ref[pl.ds(g, requests, stride=kv_heads), :] = key.astype(jnp.float32)
        u = base_value_ref[:, g * head : (g + 1) * head].astype(jnp.float32)
        u += jnp.where(lane < half, pltpu.roll(low, half, 1), high)
        value = u.astype(jnp.bfloat16)
        fresh_value_ref[:, g * head : (g + 1) * head] = value
        value_ref[pl.ds(g, requests, stride=kv_heads), :] = value.astype(jnp.float32)

    inv_sqrt = 1.0 / math.sqrt(head)
    for r in range(requests):
        query = query_ref[r * heads : (r + 1) * heads, :].astype(jnp.bfloat16)
        scores = lax.dot_general(
            query,
            keys_ref[r].reshape(kv_heads * slots, head),
            (((1,), (1,)), ((), ())),
            preferred_element_type=jnp.float32,
        )
        for g in range(kv_heads):
            score_ref[r * heads + g * group : r * heads + (g + 1) * group, :] = scores[
                g * group : (g + 1) * group, g * slots : (g + 1) * slots
            ]
    slot = lax.broadcasted_iota(jnp.int32, (heads, slots), 1)
    for r in range(requests):
        rows = slice(r * heads, (r + 1) * heads)
        query = query_ref[rows, :]
        new_key = jnp.concatenate(
            [
                jnp.broadcast_to(key_ref[r * kv_heads + g : r * kv_heads + g + 1, :], (group, head))
                for g in range(kv_heads)
            ],
            axis=0,
        )
        new_score = jnp.sum(query * new_key, axis=1, keepdims=True) * inv_sqrt
        scores = jnp.where(slot < lengths_ref[r], score_ref[rows, :] * inv_sqrt, -jnp.inf)
        row_max = jnp.maximum(jnp.max(scores, axis=1, keepdims=True), new_score)
        weights = jnp.exp(scores - row_max)
        new_weight = jnp.exp(new_score - row_max)
        total = jnp.sum(weights, axis=1, keepdims=True) + new_weight
        weight_ref[rows, :] = weights / total
        new_weight_ref[rows, :] = jnp.broadcast_to(new_weight / total, (heads, head))
    for r in range(requests):
        rows = slice(r * heads, (r + 1) * heads)
        weights = weight_ref[rows, :].astype(jnp.bfloat16)
        zero = jnp.zeros((group, slots), jnp.float32)
        wide = jnp.concatenate(
            [
                jnp.concatenate(
                    [
                        weight_ref[r * heads + g * group : r * heads + (g + 1) * group, :]
                        if o == g
                        else zero
                        for o in range(kv_heads)
                    ],
                    axis=1,
                )
                for g in range(kv_heads)
            ],
            axis=0,
        ).astype(jnp.bfloat16)
        mixed = jnp.dot(
            wide,
            values_ref[r].reshape(kv_heads * slots, head),
            preferred_element_type=jnp.float32,
        )
        new_value = jnp.concatenate(
            [
                jnp.broadcast_to(
                    value_ref[r * kv_heads + g : r * kv_heads + g + 1, :], (group, head)
                )
                for g in range(kv_heads)
            ],
            axis=0,
        )
        new_weight = new_weight_ref[rows, :].astype(jnp.bfloat16).astype(jnp.float32)
        score_ref[rows, :] = mixed + new_weight * new_value
    for h in range(heads):
        out_ref[:, h * head : (h + 1) * head] = score_ref[
            pl.ds(h, requests, stride=heads), :
        ].astype(jnp.bfloat16)


def in_smem():
    return pl.BlockSpec(memory_space=pltpu.SMEM)


def in_vmem():
    return pl.BlockSpec(memory_space=pltpu.VMEM)


def call(kernel, name, out_shape, scratch, scalars, arrays):
    return pl.pallas_call(
        kernel,
        out_shape=out_shape,
        in_specs=[in_smem()] * len(scalars) + [in_vmem()] * len(arrays),
        out_specs=[in_vmem()] * len(out_shape),
        scratch_shapes=scratch,
        compiler_params=pltpu.CompilerParams(vmem_limit_bytes=VMEM_BYTES),
        name=name,
    )(*scalars, *arrays)


def exchange(value, axis, size):
    return [value] + [
        lax.ppermute(value, axis, [(i, i ^ k) for i in range(size)]) for k in range(1, size)
    ]


def few_body(
    hidden,
    base_queries,
    base_keys,
    base_values,
    adapter_down_weight,
    adapter_up_query,
    adapter_up_key_value,
    cached_keys,
    cached_values,
    request_adapter,
    lengths,
):
    planes, columns = lax.axis_size("adapter"), lax.axis_size("tensor")
    place = lax.axis_index("adapter")
    number = place * columns + lax.axis_index("tensor")
    places = jnp.stack([place, number % planes]).astype(jnp.int32)
    requests = hidden.shape[0]
    every = requests * planes
    rank3 = adapter_down_weight.shape[1]
    head = cached_keys.shape[3]
    kv_heads = cached_keys.shape[1]
    heads = base_queries.shape[1] // head

    everyone = exchange(hidden, "adapter", planes)
    every_id = jnp.concatenate(exchange(request_adapter, "adapter", planes))[None, :]
    f32, bf16 = jnp.float32, jnp.bfloat16
    partial, every_id = call(
        down_kernel,
        "down",
        [jax.ShapeDtypeStruct((rank3, every), f32), jax.ShapeDtypeStruct((1, every), jnp.int32)],
        [pltpu.VMEM((every, hidden.shape[1]), bf16)],
        [places],
        [every_id, *everyone, adapter_down_weight],
    )
    summed = functools.reduce(jnp.add, exchange(partial, "tensor", columns)).astype(bf16)
    shrink = exchange(summed, "adapter", planes)
    width = adapter_up_query.shape[2] + 2 * adapter_up_key_value.shape[3]
    terms = call(
        up_kernel,
        "up",
        [jax.ShapeDtypeStruct((requests, width), f32)] * planes,
        [pltpu.VMEM((every, width), f32)],
        [places],
        [every_id, *shrink, adapter_up_query, adapter_up_key_value],
    )
    arrived = [
        lax.ppermute(
            term,
            ("adapter", "tensor"),
            [(n, ((n % planes) ^ k) * columns + n // planes) for n in range(planes * columns)],
        )
        for k, term in enumerate(terms)
    ]
    cosine, sine = rotation_factors(lengths, head)
    return tuple(
        call(
            attend_kernel,
            "attend",
            [
                jax.ShapeDtypeStruct(base_queries.shape, bf16),
                jax.ShapeDtypeStruct(base_keys.shape, bf16),
                jax.ShapeDtypeStruct(base_values.shape, bf16),
            ],
            [
                pltpu.VMEM((planes, requests, width), f32),
                pltpu.VMEM((requests * heads, head), f32),
                pltpu.VMEM((requests * kv_heads, head), f32),
                pltpu.VMEM((requests * kv_heads, head), f32),
                pltpu.VMEM((requests * heads, head), f32),
                pltpu.VMEM((requests * heads, head), f32),
                pltpu.VMEM((requests * heads, head), f32),
            ],
            [places, lengths],
            [*arrived, base_queries, base_keys, base_values, cosine, sine, cached_keys, cached_values],
        )
    )


def rotate_pairs(vectors, positions):
    half_dim = vectors.shape[-1] // 2
    inv_freq = jnp.exp(
        -jnp.arange(half_dim, dtype=jnp.float32) * (2.0 / vectors.shape[-1]) * math.log(ROPE_BASE)
    )
    angles = positions.astype(jnp.float32)[:, None, None] * inv_freq[None, None, :]
    cosine = jnp.cos(angles)
    sine_part = jnp.sin(angles)
    front_half = vectors[..., :half_dim]
    back_half = vectors[..., half_dim:]
    return jnp.concatenate(
        [front_half * cosine - back_half * sine_part, front_half * sine_part + back_half * cosine],
        axis=-1,
    )


def attend_cache(query_vector, key_new, value_new, cached_keys, cached_values, lengths):
    local_requests, query_heads, head_dim = query_vector.shape
    kv_heads = key_new.shape[1]
    grouped = query_vector.reshape(local_requests, kv_heads, query_heads // kv_heads, head_dim)
    inv_sqrt = 1.0 / math.sqrt(head_dim)
    cache_scores = (
        jnp.einsum("rkge,rkpe->rkgp", grouped, cached_keys, preferred_element_type=jnp.float32)
        * inv_sqrt
    )
    in_cache = jnp.arange(cached_keys.shape[2], dtype=jnp.int32)[None, :] < lengths[:, None]
    cache_scores = jnp.where(in_cache[:, None, None, :], cache_scores, -jnp.inf)
    new_score = (
        jnp.einsum("rkge,rke->rkg", grouped, key_new, preferred_element_type=jnp.float32) * inv_sqrt
    )
    row_max = jnp.maximum(jnp.max(cache_scores, axis=-1), new_score)
    cache_weights = jnp.exp(cache_scores - row_max[..., None])
    new_weight = jnp.exp(new_score - row_max)
    softmax_sum = jnp.sum(cache_weights, axis=-1) + new_weight
    cache_weights = (cache_weights / softmax_sum[..., None]).astype(jnp.bfloat16)
    new_weight = (new_weight / softmax_sum).astype(jnp.bfloat16)
    mixed = jnp.einsum(
        "rkgp,rkpe->rkge", cache_weights, cached_values, preferred_element_type=jnp.float32
    )
    mixed = (
        mixed
        + new_weight.astype(jnp.float32)[..., None] * value_new.astype(jnp.float32)[:, :, None, :]
    )
    return mixed.reshape(local_requests, query_heads * head_dim).astype(jnp.bfloat16)


def many_body(
    hidden,
    base_queries,
    base_keys,
    base_values,
    adapter_down_weight,
    adapter_up_query,
    adapter_up_key_value,
    cached_keys,
    cached_values,
    request_adapter,
    lengths,
):
    owner_index = lax.axis_index("adapter")
    owning_requests = lax.axis_size("adapter")
    holding_count = adapter_down_weight.shape[0]
    rank_width = adapter_up_query.shape[1]
    local_requests = hidden.shape[0]
    everyone, every_id = (
        lax.all_gather(hidden, "adapter", axis=0, tiled=True),
        lax.all_gather(request_adapter, "adapter", axis=0, tiled=True),
    )
    every_row = everyone.shape[0]
    slot_of = every_id - owner_index * holding_count
    picked = slot_of[:, None] == jnp.arange(holding_count, dtype=jnp.int32)[None, :]
    picked_float = picked.astype(jnp.float32)
    flattened_lowered = adapter_down_weight.reshape(
        holding_count * 3 * rank_width, adapter_down_weight.shape[2]
    )
    partial_value = lax.dot_general(
        everyone, flattened_lowered, (((1,), (1,)), ((), ())), preferred_element_type=jnp.float32
    )
    summed = lax.psum(partial_value, "tensor")
    mine = jnp.sum(
        summed.reshape(every_row, holding_count, 3 * rank_width) * picked_float[:, :, None], axis=1
    )
    shrink_rank = lax.psum(mine.astype(jnp.bfloat16), "adapter").astype(jnp.float32)
    shrink_rank = shrink_rank.astype(jnp.bfloat16)

    def expand_rank(segment, factors):
        rows_used = jnp.take(factors, every_id, axis=0)
        rank_product = jnp.einsum(
            "rj,rjc->rc", segment, rows_used, preferred_element_type=jnp.float32
        )
        column_width = rank_product.shape[1]
        return (ADAPTER_SCALE * rank_product).reshape(
            owning_requests, every_row // owning_requests, 1, column_width
        )

    query_portion = expand_rank(shrink_rank[:, :rank_width], adapter_up_query)
    key_portion = expand_rank(
        shrink_rank[:, rank_width : 2 * rank_width], adapter_up_key_value[:, 0]
    )
    value_portion = expand_rank(shrink_rank[:, 2 * rank_width :], adapter_up_key_value[:, 1])
    arrived = (
        lax.all_to_all(
            lax.all_to_all(query_portion, "adapter", split_axis=0, concat_axis=2, tiled=True),
            "tensor",
            split_axis=2,
            concat_axis=0,
            tiled=True,
        ),
        lax.all_to_all(
            lax.all_to_all(key_portion, "adapter", split_axis=0, concat_axis=2, tiled=True),
            "tensor",
            split_axis=2,
            concat_axis=0,
            tiled=True,
        ),
        lax.all_to_all(
            lax.all_to_all(value_portion, "adapter", split_axis=0, concat_axis=2, tiled=True),
            "tensor",
            split_axis=2,
            concat_axis=0,
            tiled=True,
        ),
    )

    def columns(values):
        return jnp.transpose(values, (1, 2, 0, 3)).reshape(local_requests, -1)

    query_update = columns(arrived[0])
    key_update = columns(arrived[1])
    value_update = columns(arrived[2])
    head_dim = cached_keys.shape[3]
    kv_heads = cached_keys.shape[1]
    query_heads = base_queries.shape[1] // head_dim
    query_vector = rotate_pairs(
        (base_queries.astype(jnp.float32) + query_update).reshape(
            local_requests, query_heads, head_dim
        ),
        lengths,
    ).astype(jnp.bfloat16)
    fresh_keys = rotate_pairs(
        (base_keys.astype(jnp.float32) + key_update).reshape(local_requests, kv_heads, head_dim),
        lengths,
    ).astype(jnp.bfloat16)
    fresh_values = (base_values.astype(jnp.float32) + value_update).astype(jnp.bfloat16)
    attention = attend_cache(
        query_vector,
        fresh_keys,
        fresh_values.reshape(local_requests, kv_heads, head_dim),
        cached_keys,
        cached_values,
        lengths,
    )
    return (attention, fresh_keys.reshape(local_requests, kv_heads * head_dim), fresh_values)


def solution(mesh):
    few = mesh.shape["adapter"] == 4 and mesh.shape["tensor"] == 4
    return jax.shard_map(
        few_body if few else many_body,
        mesh=mesh,
        in_specs=(
            P(("groups", "adapter"), "tensor"),
            P(("groups", "adapter"), "tensor"),
            P(("groups", "adapter"), "tensor"),
            P(("groups", "adapter"), "tensor"),
            P("adapter", None, "tensor"),
            P(None, None, ("adapter", "tensor")),
            P(None, None, None, ("adapter", "tensor")),
            P(("groups", "adapter"), "tensor", None, None),
            P(("groups", "adapter"), "tensor", None, None),
            P(("groups", "adapter")),
            P(("groups", "adapter")),
        ),
        out_specs=(
            P(("groups", "adapter"), "tensor"),
            P(("groups", "adapter"), "tensor"),
            P(("groups", "adapter"), "tensor"),
        ),
        check_vma=False,
    )
```

```python
import functools
import math

import jax
import jax.numpy as jnp
from jax import lax
from jax.experimental import pallas as pl
from jax.experimental.pallas import tpu as pltpu
from jax.sharding import PartitionSpec as P

ADAPTER_SCALE = 0.5
ROPE_BASE = 500000.0
LANES = 128
VMEM_BYTES = 16 * 1024 * 1024
LOAD_BYTES = 52 * 1024 * 1024
PACK_BYTES = 60 * 1024 * 1024


def rotation_factors(positions, head_dim):
    half_dim = head_dim // 2
    inv_freq = jnp.exp(
        -jnp.arange(half_dim, dtype=jnp.float32) * (2.0 / head_dim) * math.log(ROPE_BASE)
    )
    angles = positions.astype(jnp.float32)[:, None] * inv_freq[None, :]
    return jnp.cos(angles), jnp.sin(angles)


def pack_kernel(ids_in, hidden_in, out_ref, ids_ref, sems):
    requests, width = hidden_in.shape
    ids_copy = pltpu.make_async_copy(ids_in, ids_ref, sems.at[0])
    hidden_copy = pltpu.make_async_copy(hidden_in, out_ref.at[:, pl.ds(0, width)], sems.at[1])
    hidden_copy.start()
    ids_copy.start()
    ids_copy.wait()
    row = lax.broadcasted_iota(jnp.int32, (requests, LANES), 0)
    ids = jnp.zeros((requests, LANES), jnp.int32)
    for r in range(requests):
        ids = jnp.where(row == r, ids_ref[r], ids)
    out_ref[:, width:] = ids.astype(jnp.float32).astype(jnp.bfloat16)
    hidden_copy.wait()


def pack(request_adapter, hidden):
    requests, width = hidden.shape
    return pl.pallas_call(
        pack_kernel,
        out_shape=pltpu.VMEM((requests, width + LANES), jnp.bfloat16),
        in_specs=[pl.BlockSpec(memory_space=pltpu.HBM)] * 2,
        out_specs=in_vmem(),
        scratch_shapes=[
            pltpu.SMEM(request_adapter.shape, jnp.int32),
            pltpu.SemaphoreType.DMA((2,)),
        ],
        compiler_params=pltpu.CompilerParams(vmem_limit_bytes=PACK_BYTES),
        name="pack",
    )(request_adapter, hidden)


def down_kernel(place_ref, *refs):
    *message_refs, down_ref, out_ref, ids_ref, rows_ref = refs
    place = place_ref[0]
    held, rank, width = down_ref.shape
    block = message_refs[0].shape[0]
    for k, message_ref in zip((0, 3, 2, 1), message_refs):
        start = pl.multiple_of((place ^ k) * block, block)
        rows_ref[pl.ds(start, block), :] = message_ref[...]
    ids = rows_ref[:, width:].astype(jnp.float32)
    ids_ref[...] = ids
    slot = jnp.transpose(ids)[0:1] - (place * held).astype(jnp.float32)
    product = lax.dot_general(
        down_ref[...].reshape(held * rank, width),
        rows_ref[:, :width],
        (((1,), (1,)), ((), ())),
        preferred_element_type=jnp.float32,
    )
    total = jnp.zeros(out_ref.shape, jnp.float32)
    for s in range(held):
        total += jnp.where(slot == s, product[s * rank : (s + 1) * rank], 0.0)
    out_ref[...] = total


def up_kernel(place_ref, ids_ref, *refs):
    shrink_refs = refs[:4]
    up_query_ref, up_kv_ref, *out_refs, terms_ref = refs[4:]
    shrink = shrink_refs[0][...].astype(jnp.float32)
    for ref in shrink_refs[1:]:
        shrink += ref[...].astype(jnp.float32)
    rank = shrink.shape[0] // 3
    rows = shrink.shape[1]
    shrink = jnp.concatenate([shrink, jnp.zeros((LANES - 3 * rank, rows), jnp.float32)], axis=0)
    shrink = jnp.transpose(shrink)
    ids = ids_ref[...]
    lane = lax.broadcasted_iota(jnp.int32, (rows, LANES), 1)
    count = up_query_ref.shape[0]
    query = jnp.concatenate([shrink[:, :rank]] * (LANES // rank), axis=1)
    lane_slot = (lane // rank).astype(jnp.float32)
    step = LANES // rank
    spread = jnp.concatenate(
        [
            jnp.where(ids - c * step == lane_slot, query, 0.0).astype(jnp.bfloat16)
            for c in range(count // step)
        ],
        axis=1,
    )
    terms_ref[:, : up_query_ref.shape[2]] = ADAPTER_SCALE * jnp.dot(
        spread,
        up_query_ref[...].reshape(count * rank, up_query_ref.shape[2]),
        preferred_element_type=jnp.float32,
    )
    pair = jnp.concatenate([shrink[:, rank : 3 * rank]] * (LANES // (2 * rank)), axis=1)
    lane_slot = (lane // (2 * rank)).astype(jnp.float32)
    is_key = (lane // rank) % 2 == 0
    key, value = jnp.where(is_key, pair, 0.0), jnp.where(is_key, 0.0, pair)
    step = LANES // (2 * rank)
    both = []
    for part in (key, value):
        both.append(
            jnp.concatenate(
                [
                    jnp.where(ids - c * step == lane_slot, part, 0.0).astype(jnp.bfloat16)
                    for c in range(count // step)
                ],
                axis=1,
            )
        )
    kv_width = up_kv_ref.shape[3]
    kv = ADAPTER_SCALE * jnp.dot(
        jnp.concatenate(both, axis=0),
        up_kv_ref[...].reshape(count * 2 * rank, kv_width),
        preferred_element_type=jnp.float32,
    )
    terms_ref[:, up_query_ref.shape[2] :] = jnp.concatenate([kv[:rows], kv[rows:]], axis=1)
    block = out_refs[0].shape[0]
    for k, out_ref in enumerate(out_refs):
        start = pl.multiple_of((place_ref[1] ^ k) * block, block)
        out_ref[...] = terms_ref[pl.ds(start, block), :]


def attend_kernel(place_ref, lengths_ref, *refs):
    term_refs = refs[:4]
    (
        base_query_ref,
        base_key_ref,
        base_value_ref,
        cosine_ref,
        sine_ref,
        keys_ref,
        values_ref,
        out_ref,
        fresh_key_ref,
        fresh_value_ref,
        terms_ref,
        query_ref,
        key_ref,
        value_ref,
        score_ref,
        weight_ref,
        new_weight_ref,
    ) = refs[4:]
    place = place_ref[0]
    for k, term_ref in enumerate(term_refs):
        terms_ref[place ^ k] = term_ref[...]
    requests = base_query_ref.shape[0]
    kv_heads = keys_ref.shape[1]
    slots, head = keys_ref.shape[2], keys_ref.shape[3]
    half = head // 2
    heads = base_query_ref.shape[1] // head
    group = heads // kv_heads
    each = terms_ref.shape[2] // head - 1
    cosine, sine = cosine_ref[...], sine_ref[...]
    lane = lax.broadcasted_iota(jnp.int32, (requests, head), 1)
    cosine = jnp.concatenate([cosine, cosine], axis=1)
    sine = jnp.concatenate([-sine, sine], axis=1)

    def rotate(u):
        return (u * cosine + pltpu.roll(u, half, 1) * sine).astype(jnp.bfloat16)

    for h in range(heads):
        c = (h % each) * head
        u = base_query_ref[:, h * head : (h + 1) * head].astype(jnp.float32)
        u += terms_ref[h // each, :, c : c + head]
        query_ref[pl.ds(h, requests, stride=heads), :] = rotate(u).astype(jnp.float32)
    for g in range(kv_heads):
        low = terms_ref[2 * g, :, each * head :]
        high = terms_ref[2 * g + 1, :, each * head :]
        u = base_key_ref[:, g * head : (g + 1) * head].astype(jnp.float32)
        u += jnp.where(lane < half, low, pltpu.roll(high, half, 1))
        key = rotate(u)
        fresh_key_ref[:, g * head : (g + 1) * head] = key
        key_ref[pl.ds(g, requests, stride=kv_heads), :] = key.astype(jnp.float32)
        u = base_value_ref[:, g * head : (g + 1) * head].astype(jnp.float32)
        u += jnp.where(lane < half, pltpu.roll(low, half, 1), high)
        value = u.astype(jnp.bfloat16)
        fresh_value_ref[:, g * head : (g + 1) * head] = value
        value_ref[pl.ds(g, requests, stride=kv_heads), :] = value.astype(jnp.float32)

    inv_sqrt = 1.0 / math.sqrt(head)
    for r in range(requests):
        query = query_ref[r * heads : (r + 1) * heads, :].astype(jnp.bfloat16)
        scores = lax.dot_general(
            query,
            keys_ref[r].reshape(kv_heads * slots, head),
            (((1,), (1,)), ((), ())),
            preferred_element_type=jnp.float32,
        )
        for g in range(kv_heads):
            score_ref[r * heads + g * group : r * heads + (g + 1) * group, :] = scores[
                g * group : (g + 1) * group, g * slots : (g + 1) * slots
            ]
    slot = lax.broadcasted_iota(jnp.int32, (heads, slots), 1)
    for r in range(requests):
        rows = slice(r * heads, (r + 1) * heads)
        query = query_ref[rows, :]
        new_key = jnp.concatenate(
            [
                jnp.broadcast_to(key_ref[r * kv_heads + g : r * kv_heads + g + 1, :], (group, head))
                for g in range(kv_heads)
            ],
            axis=0,
        )
        new_score = jnp.sum(query * new_key, axis=1, keepdims=True) * inv_sqrt
        scores = jnp.where(slot < lengths_ref[r], score_ref[rows, :] * inv_sqrt, -jnp.inf)
        row_max = jnp.maximum(jnp.max(scores, axis=1, keepdims=True), new_score)
        weights = jnp.exp(scores - row_max)
        new_weight = jnp.exp(new_score - row_max)
        total = jnp.sum(weights, axis=1, keepdims=True) + new_weight
        weight_ref[rows, :] = weights / total
        new_weight_ref[rows, :] = jnp.broadcast_to(new_weight / total, (heads, head))
    for r in range(requests):
        rows = slice(r * heads, (r + 1) * heads)
        weights = weight_ref[rows, :].astype(jnp.bfloat16)
        zero = jnp.zeros((group, slots), jnp.float32)
        wide = jnp.concatenate(
            [
                jnp.concatenate(
                    [
                        weight_ref[r * heads + g * group : r * heads + (g + 1) * group, :]
                        if o == g
                        else zero
                        for o in range(kv_heads)
                    ],
                    axis=1,
                )
                for g in range(kv_heads)
            ],
            axis=0,
        ).astype(jnp.bfloat16)
        mixed = jnp.dot(
            wide,
            values_ref[r].reshape(kv_heads * slots, head),
            preferred_element_type=jnp.float32,
        )
        new_value = jnp.concatenate(
            [
                jnp.broadcast_to(
                    value_ref[r * kv_heads + g : r * kv_heads + g + 1, :], (group, head)
                )
                for g in range(kv_heads)
            ],
            axis=0,
        )
        new_weight = new_weight_ref[rows, :].astype(jnp.bfloat16).astype(jnp.float32)
        score_ref[rows, :] = mixed + new_weight * new_value
    for h in range(heads):
        out_ref[:, h * head : (h + 1) * head] = score_ref[
            pl.ds(h, requests, stride=heads), :
        ].astype(jnp.bfloat16)


def load_kernel(*refs):
    count = (len(refs) - 1) // 2
    sems = refs[-1]
    copies = [
        pltpu.make_async_copy(refs[i], refs[count + i], sems.at[i]) for i in range(count)
    ]
    for copy in copies:
        copy.start()
    for copy in copies:
        copy.wait()


def load(arrays):
    return pl.pallas_call(
        load_kernel,
        out_shape=[pltpu.VMEM(a.shape, a.dtype) for a in arrays],
        in_specs=[pl.BlockSpec(memory_space=pltpu.HBM)] * len(arrays),
        out_specs=[in_vmem()] * len(arrays),
        scratch_shapes=[pltpu.SemaphoreType.DMA((len(arrays),))],
        compiler_params=pltpu.CompilerParams(vmem_limit_bytes=LOAD_BYTES),
        cost_estimate=pl.CostEstimate(
            flops=0, bytes_accessed=sum(a.size for a in arrays) * 4, transcendentals=0
        ),
        name="load",
    )(*arrays)


def in_smem():
    return pl.BlockSpec(memory_space=pltpu.SMEM)


def in_vmem():
    return pl.BlockSpec(memory_space=pltpu.VMEM)


def call(kernel, name, out_shape, scratch, scalars, arrays):
    return pl.pallas_call(
        kernel,
        out_shape=out_shape,
        in_specs=[in_smem()] * len(scalars) + [in_vmem()] * len(arrays),
        out_specs=[in_vmem()] * len(out_shape),
        scratch_shapes=scratch,
        compiler_params=pltpu.CompilerParams(vmem_limit_bytes=VMEM_BYTES),
        name=name,
    )(*scalars, *arrays)


def step(value, axis, size, k):
    return lax.ppermute(value, axis, [(i, i ^ k) for i in range(size)])


def exchange(value, axis, size):
    return [value] + [step(value, axis, size, k) for k in range(size - 1, 0, -1)]


def few_body(
    hidden,
    base_queries,
    base_keys,
    base_values,
    adapter_down_weight,
    adapter_up_query,
    adapter_up_key_value,
    cached_keys,
    cached_values,
    request_adapter,
    lengths,
):
    planes, columns = lax.axis_size("adapter"), lax.axis_size("tensor")
    place = lax.axis_index("adapter")
    number = place * columns + lax.axis_index("tensor")
    places = jnp.stack([place, number % planes]).astype(jnp.int32)
    requests = hidden.shape[0]
    every = requests * planes
    rank3 = adapter_down_weight.shape[1]
    head = cached_keys.shape[3]
    kv_heads = cached_keys.shape[1]
    heads = base_queries.shape[1] // head

    f32, bf16 = jnp.float32, jnp.bfloat16
    message = pack(request_adapter, hidden)
    mirror = step(message, "adapter", planes, planes - 1)
    near = step(message, "adapter", planes, 1)
    everyone = [message, mirror, step(mirror, "adapter", planes, 1), near]
    (
        adapter_down_weight,
        adapter_up_query,
        adapter_up_key_value,
        base_queries,
        base_keys,
        base_values,
        cached_keys,
        cached_values,
    ) = load(
        [
            adapter_down_weight,
            adapter_up_query,
            adapter_up_key_value,
            base_queries,
            base_keys,
            base_values,
            cached_keys,
            cached_values,
        ]
    )
    partial, every_id = call(
        down_kernel,
        "down",
        [jax.ShapeDtypeStruct((rank3, every), f32), jax.ShapeDtypeStruct((every, LANES), f32)],
        [pltpu.VMEM((every, hidden.shape[1] + LANES), bf16)],
        [places],
        [*everyone, adapter_down_weight],
    )
    summed = functools.reduce(jnp.add, exchange(partial, "tensor", columns)).astype(bf16)
    shrink = exchange(summed, "adapter", planes)
    width = adapter_up_query.shape[2] + 2 * adapter_up_key_value.shape[3]
    terms = call(
        up_kernel,
        "up",
        [jax.ShapeDtypeStruct((requests, width), f32)] * planes,
        [pltpu.VMEM((every, width), f32)],
        [places],
        [every_id, *shrink, adapter_up_query, adapter_up_key_value],
    )
    arrived = [
        lax.ppermute(
            term,
            ("adapter", "tensor"),
            [(n, ((n % planes) ^ k) * columns + n // planes) for n in range(planes * columns)],
        )
        for k, term in enumerate(terms)
    ]
    cosine, sine = rotation_factors(lengths, head)
    return tuple(
        call(
            attend_kernel,
            "attend",
            [
                jax.ShapeDtypeStruct(base_queries.shape, bf16),
                jax.ShapeDtypeStruct(base_keys.shape, bf16),
                jax.ShapeDtypeStruct(base_values.shape, bf16),
            ],
            [
                pltpu.VMEM((planes, requests, width), f32),
                pltpu.VMEM((requests * heads, head), f32),
                pltpu.VMEM((requests * kv_heads, head), f32),
                pltpu.VMEM((requests * kv_heads, head), f32),
                pltpu.VMEM((requests * heads, head), f32),
                pltpu.VMEM((requests * heads, head), f32),
                pltpu.VMEM((requests * heads, head), f32),
            ],
            [places, lengths],
            [*arrived, base_queries, base_keys, base_values, cosine, sine, cached_keys, cached_values],
        )
    )


def rotate_pairs(vectors, positions):
    half_dim = vectors.shape[-1] // 2
    inv_freq = jnp.exp(
        -jnp.arange(half_dim, dtype=jnp.float32) * (2.0 / vectors.shape[-1]) * math.log(ROPE_BASE)
    )
    angles = positions.astype(jnp.float32)[:, None, None] * inv_freq[None, None, :]
    cosine = jnp.cos(angles)
    sine_part = jnp.sin(angles)
    front_half = vectors[..., :half_dim]
    back_half = vectors[..., half_dim:]
    return jnp.concatenate(
        [front_half * cosine - back_half * sine_part, front_half * sine_part + back_half * cosine],
        axis=-1,
    )


def attend_cache(query_vector, key_new, value_new, cached_keys, cached_values, lengths):
    local_requests, query_heads, head_dim = query_vector.shape
    kv_heads = key_new.shape[1]
    grouped = query_vector.reshape(local_requests, kv_heads, query_heads // kv_heads, head_dim)
    inv_sqrt = 1.0 / math.sqrt(head_dim)
    cache_scores = (
        jnp.einsum("rkge,rkpe->rkgp", grouped, cached_keys, preferred_element_type=jnp.float32)
        * inv_sqrt
    )
    in_cache = jnp.arange(cached_keys.shape[2], dtype=jnp.int32)[None, :] < lengths[:, None]
    cache_scores = jnp.where(in_cache[:, None, None, :], cache_scores, -jnp.inf)
    new_score = (
        jnp.einsum("rkge,rke->rkg", grouped, key_new, preferred_element_type=jnp.float32) * inv_sqrt
    )
    row_max = jnp.maximum(jnp.max(cache_scores, axis=-1), new_score)
    cache_weights = jnp.exp(cache_scores - row_max[..., None])
    new_weight = jnp.exp(new_score - row_max)
    softmax_sum = jnp.sum(cache_weights, axis=-1) + new_weight
    cache_weights = (cache_weights / softmax_sum[..., None]).astype(jnp.bfloat16)
    new_weight = (new_weight / softmax_sum).astype(jnp.bfloat16)
    mixed = jnp.einsum(
        "rkgp,rkpe->rkge", cache_weights, cached_values, preferred_element_type=jnp.float32
    )
    mixed = (
        mixed
        + new_weight.astype(jnp.float32)[..., None] * value_new.astype(jnp.float32)[:, :, None, :]
    )
    return mixed.reshape(local_requests, query_heads * head_dim).astype(jnp.bfloat16)


def many_body(
    hidden,
    base_queries,
    base_keys,
    base_values,
    adapter_down_weight,
    adapter_up_query,
    adapter_up_key_value,
    cached_keys,
    cached_values,
    request_adapter,
    lengths,
):
    owner_index = lax.axis_index("adapter")
    owning_requests = lax.axis_size("adapter")
    holding_count = adapter_down_weight.shape[0]
    rank_width = adapter_up_query.shape[1]
    local_requests = hidden.shape[0]
    everyone, every_id = (
        lax.all_gather(hidden, "adapter", axis=0, tiled=True),
        lax.all_gather(request_adapter, "adapter", axis=0, tiled=True),
    )
    every_row = everyone.shape[0]
    slot_of = every_id - owner_index * holding_count
    picked = slot_of[:, None] == jnp.arange(holding_count, dtype=jnp.int32)[None, :]
    picked_float = picked.astype(jnp.float32)
    flattened_lowered = adapter_down_weight.reshape(
        holding_count * 3 * rank_width, adapter_down_weight.shape[2]
    )
    partial_value = lax.dot_general(
        everyone, flattened_lowered, (((1,), (1,)), ((), ())), preferred_element_type=jnp.float32
    )
    summed = lax.psum(partial_value, "tensor")
    mine = jnp.sum(
        summed.reshape(every_row, holding_count, 3 * rank_width) * picked_float[:, :, None], axis=1
    )
    shrink_rank = lax.psum(mine.astype(jnp.bfloat16), "adapter").astype(jnp.float32)
    shrink_rank = shrink_rank.astype(jnp.bfloat16)

    def expand_rank(segment, factors):
        rows_used = jnp.take(factors, every_id, axis=0)
        rank_product = jnp.einsum(
            "rj,rjc->rc", segment, rows_used, preferred_element_type=jnp.float32
        )
        column_width = rank_product.shape[1]
        return (ADAPTER_SCALE * rank_product).reshape(
            owning_requests, every_row // owning_requests, 1, column_width
        )

    query_portion = expand_rank(shrink_rank[:, :rank_width], adapter_up_query)
    key_portion = expand_rank(
        shrink_rank[:, rank_width : 2 * rank_width], adapter_up_key_value[:, 0]
    )
    value_portion = expand_rank(shrink_rank[:, 2 * rank_width :], adapter_up_key_value[:, 1])
    arrived = (
        lax.all_to_all(
            lax.all_to_all(query_portion, "adapter", split_axis=0, concat_axis=2, tiled=True),
            "tensor",
            split_axis=2,
            concat_axis=0,
            tiled=True,
        ),
        lax.all_to_all(
            lax.all_to_all(key_portion, "adapter", split_axis=0, concat_axis=2, tiled=True),
            "tensor",
            split_axis=2,
            concat_axis=0,
            tiled=True,
        ),
        lax.all_to_all(
            lax.all_to_all(value_portion, "adapter", split_axis=0, concat_axis=2, tiled=True),
            "tensor",
            split_axis=2,
            concat_axis=0,
            tiled=True,
        ),
    )

    def columns(values):
        return jnp.transpose(values, (1, 2, 0, 3)).reshape(local_requests, -1)

    query_update = columns(arrived[0])
    key_update = columns(arrived[1])
    value_update = columns(arrived[2])
    head_dim = cached_keys.shape[3]
    kv_heads = cached_keys.shape[1]
    query_heads = base_queries.shape[1] // head_dim
    query_vector = rotate_pairs(
        (base_queries.astype(jnp.float32) + query_update).reshape(
            local_requests, query_heads, head_dim
        ),
        lengths,
    ).astype(jnp.bfloat16)
    fresh_keys = rotate_pairs(
        (base_keys.astype(jnp.float32) + key_update).reshape(local_requests, kv_heads, head_dim),
        lengths,
    ).astype(jnp.bfloat16)
    fresh_values = (base_values.astype(jnp.float32) + value_update).astype(jnp.bfloat16)
    attention = attend_cache(
        query_vector,
        fresh_keys,
        fresh_values.reshape(local_requests, kv_heads, head_dim),
        cached_keys,
        cached_values,
        lengths,
    )
    return (attention, fresh_keys.reshape(local_requests, kv_heads * head_dim), fresh_values)


def solution(mesh):
    few = mesh.shape["adapter"] == 4 and mesh.shape["tensor"] == 4
    return jax.shard_map(
        few_body if few else many_body,
        mesh=mesh,
        in_specs=(
            P(("groups", "adapter"), "tensor"),
            P(("groups", "adapter"), "tensor"),
            P(("groups", "adapter"), "tensor"),
            P(("groups", "adapter"), "tensor"),
            P("adapter", None, "tensor"),
            P(None, None, ("adapter", "tensor")),
            P(None, None, None, ("adapter", "tensor")),
            P(("groups", "adapter"), "tensor", None, None),
            P(("groups", "adapter"), "tensor", None, None),
            P(("groups", "adapter")),
            P(("groups", "adapter")),
        ),
        out_specs=(
            P(("groups", "adapter"), "tensor"),
            P(("groups", "adapter"), "tensor"),
            P(("groups", "adapter"), "tensor"),
        ),
        check_vma=False,
    )
```

```python
import functools
import math

import jax
import jax.numpy as jnp
from jax import lax
from jax.experimental import pallas as pl
from jax.experimental.pallas import tpu as pltpu
from jax.sharding import PartitionSpec as P

ADAPTER_SCALE = 0.5
ROPE_BASE = 500000.0
LANES = 128
VMEM_BYTES = 16 * 1024 * 1024
LOAD_BYTES = 52 * 1024 * 1024
PACK_BYTES = 60 * 1024 * 1024


def rotation_factors(positions, head_dim):
    half_dim = head_dim // 2
    inv_freq = jnp.exp(
        -jnp.arange(half_dim, dtype=jnp.float32) * (2.0 / head_dim) * math.log(ROPE_BASE)
    )
    angles = positions.astype(jnp.float32)[:, None] * inv_freq[None, :]
    return jnp.cos(angles), jnp.sin(angles)


FLIPS = 0b1111


def position():
    column = lax.axis_index("tensor")
    return lax.axis_index("adapter"), column % 2, column // 2


def plane_of(core, index):
    return (3 * index) ^ core


def core_of(plane):
    return (plane ^ (plane >> 1)) & 1


def index_of(plane):
    return plane >> 1


def flip_of(plane, core):
    return (FLIPS >> (2 * plane + core)) & 1


def pack_kernel(ids_in, hidden_in, out_ref, ids_ref, sems):
    requests, width = hidden_in.shape
    ids_copy = pltpu.make_async_copy(ids_in, ids_ref, sems.at[0])
    hidden_copy = pltpu.make_async_copy(hidden_in, out_ref.at[:, pl.ds(0, width)], sems.at[1])
    hidden_copy.start()
    ids_copy.start()
    ids_copy.wait()
    row = lax.broadcasted_iota(jnp.int32, (requests, LANES), 0)
    ids = jnp.zeros((requests, LANES), jnp.int32)
    for r in range(requests):
        ids = jnp.where(row == r, ids_ref[r], ids)
    out_ref[:, width:] = ids.astype(jnp.float32).astype(jnp.bfloat16)
    hidden_copy.wait()


def pack(request_adapter, hidden):
    requests, width = hidden.shape
    return pl.pallas_call(
        pack_kernel,
        out_shape=pltpu.VMEM((requests, width + LANES), jnp.bfloat16),
        in_specs=[pl.BlockSpec(memory_space=pltpu.HBM)] * 2,
        out_specs=in_vmem(),
        scratch_shapes=[
            pltpu.SMEM(request_adapter.shape, jnp.int32),
            pltpu.SemaphoreType.DMA((2,)),
        ],
        compiler_params=pltpu.CompilerParams(vmem_limit_bytes=PACK_BYTES),
        name="pack",
    )(request_adapter, hidden)


def down_kernel(*refs):
    *message_refs, down_ref, out_ref, ids_ref, rows_ref = refs
    place = position()[0]
    held, rank, width = down_ref.shape
    block = message_refs[0].shape[0]
    for k, message_ref in zip((0, 3, 2, 1), message_refs):
        start = pl.multiple_of((place ^ k) * block, block)
        rows_ref[pl.ds(start, block), :] = message_ref[...]
    ids = rows_ref[:, width:].astype(jnp.float32)
    ids_ref[...] = ids
    slot = jnp.transpose(ids)[0:1] - (place * held).astype(jnp.float32)
    product = lax.dot_general(
        down_ref[...].reshape(held * rank, width),
        rows_ref[:, :width],
        (((1,), (1,)), ((), ())),
        preferred_element_type=jnp.float32,
    )
    total = jnp.zeros(out_ref.shape, jnp.float32)
    for s in range(held):
        total += jnp.where(slot == s, product[s * rank : (s + 1) * rank], 0.0)
    out_ref[...] = total


def up_kernel(ids_ref, *refs):
    shrink_refs, query_refs, kv_refs = refs[:4], refs[4:6], refs[6:8]
    *out_refs, rows_ref, terms_ref = refs[8:]
    place, core, side = position()
    side ^= flip_of(place, core)
    shrink = shrink_refs[0][...].astype(jnp.float32)
    for ref in shrink_refs[1:]:
        shrink += ref[...].astype(jnp.float32)
    rank = shrink.shape[0] // 3
    every = shrink.shape[1]
    shrink = jnp.concatenate([shrink, jnp.zeros((LANES - 3 * rank, every), jnp.float32)], axis=0)
    rows_ref[...] = jnp.transpose(shrink)
    rows = every // 2
    block = out_refs[0].shape[0]
    starts = [pl.multiple_of(plane_of(core, i) * block, block) for i in range(2)]
    shrink = jnp.concatenate([rows_ref[pl.ds(start, block), :] for start in starts], axis=0)
    ids = jnp.concatenate([ids_ref[pl.ds(start, block), :] for start in starts], axis=0)
    lane = lax.broadcasted_iota(jnp.int32, (rows, LANES), 1)
    count = query_refs[0].shape[0]

    def spread(part, width):
        slot = (lane // width).astype(jnp.float32)
        each = LANES // width
        return jnp.concatenate(
            [
                jnp.where(ids - c * each == slot, part, 0.0).astype(jnp.bfloat16)
                for c in range(count // each)
            ],
            axis=1,
        )

    query = spread(jnp.concatenate([shrink[:, :rank]] * (LANES // rank), axis=1), rank)
    pair = jnp.concatenate([shrink[:, rank : 3 * rank]] * (LANES // (2 * rank)), axis=1)
    is_key = (lane // rank) % 2 == 0
    pair = jnp.concatenate(
        [
            spread(jnp.where(is_key, pair, 0.0), 2 * rank),
            spread(jnp.where(is_key, 0.0, pair), 2 * rank),
        ],
        axis=0,
    )
    width = query_refs[0].shape[2]
    half = kv_refs[0].shape[3]
    kv = []
    for which in range(2):
        column = pl.multiple_of((core ^ which) * width, width)
        terms_ref[:, pl.ds(column, width)] = ADAPTER_SCALE * jnp.dot(
            query,
            query_refs[which][...].reshape(count * rank, width),
            preferred_element_type=jnp.float32,
        )
        kv.append(
            ADAPTER_SCALE
            * jnp.dot(
                pair,
                kv_refs[which][...].reshape(count * 2 * rank, half),
                preferred_element_type=jnp.float32,
            )
        )
    both = jnp.concatenate(kv, axis=1)
    both = jnp.where(core == 0, both, pltpu.roll(both, half, 1))
    terms_ref[:, 2 * width : 2 * width + LANES] = both[:rows]
    terms_ref[:, 2 * width + LANES :] = both[rows:]
    terms = terms_ref[...]
    largest = jnp.max(jnp.abs(terms), axis=1, keepdims=True)
    power = jnp.clip(jnp.ceil(jnp.log2(jnp.maximum(largest, 1e-30))), -100.0, 100.0)
    terms_ref[...] = terms * jnp.exp2(-power)
    total = terms.shape[1]
    for k, out_ref in enumerate(out_refs):
        at = pl.multiple_of((side ^ k) * block, block)
        out_ref[:, :total] = terms_ref[pl.ds(at, block), :]
        out_ref[:, total:] = jnp.broadcast_to(
            jnp.where((side ^ k) == 0, power[:block], power[block:]), (block, LANES)
        )


def attend_kernel(*refs):
    term_refs = refs[:2]
    (
        base_query_ref,
        base_key_ref,
        base_value_ref,
        lengths_ref,
        cosine_ref,
        sine_ref,
        keys_ref,
        values_ref,
        out_ref,
        fresh_key_ref,
        fresh_value_ref,
        terms_ref,
        query_ref,
        key_ref,
        value_ref,
        score_ref,
        weight_ref,
        new_weight_ref,
    ) = refs[2:]
    place, core, side = position()
    odd = index_of(place) ^ flip_of(2 * side + core, core_of(place))
    total = terms_ref.shape[2]
    for k, term_ref in enumerate(term_refs):
        scale = jnp.exp2(term_ref[:, total : total + 1])
        terms_ref[odd ^ k] = term_ref[:, :total] * scale
    requests = base_query_ref.shape[0]
    kv_heads = keys_ref.shape[1]
    slots, head = keys_ref.shape[2], keys_ref.shape[3]
    half = head // 2
    heads = base_query_ref.shape[1] // head
    group = heads // kv_heads
    wide = group * head
    cosine, sine = cosine_ref[...], sine_ref[...]
    cosine = jnp.concatenate([cosine, cosine], axis=1)
    sine = jnp.concatenate([-sine, sine], axis=1)

    def rotate(u):
        return (u * cosine + pltpu.roll(u, half, 1) * sine).astype(jnp.bfloat16)

    for h in range(heads):
        c = (h % group) * head
        u = base_query_ref[:, h * head : (h + 1) * head].astype(jnp.float32)
        u += terms_ref[h // group, :, c : c + head]
        query_ref[pl.ds(h, requests, stride=heads), :] = rotate(u).astype(jnp.float32)
    for g in range(kv_heads):
        u = base_key_ref[:, g * head : (g + 1) * head].astype(jnp.float32)
        key = rotate(u + terms_ref[g, :, wide : wide + head])
        fresh_key_ref[:, g * head : (g + 1) * head] = key
        key_ref[pl.ds(g, requests, stride=kv_heads), :] = key.astype(jnp.float32)
        u = base_value_ref[:, g * head : (g + 1) * head].astype(jnp.float32)
        value = (u + terms_ref[g, :, wide + head :]).astype(jnp.bfloat16)
        fresh_value_ref[:, g * head : (g + 1) * head] = value
        value_ref[pl.ds(g, requests, stride=kv_heads), :] = value.astype(jnp.float32)

    inv_sqrt = 1.0 / math.sqrt(head)
    for r in range(requests):
        query = query_ref[r * heads : (r + 1) * heads, :].astype(jnp.bfloat16)
        scores = lax.dot_general(
            query,
            keys_ref[r].reshape(kv_heads * slots, head),
            (((1,), (1,)), ((), ())),
            preferred_element_type=jnp.float32,
        )
        for g in range(kv_heads):
            score_ref[r * heads + g * group : r * heads + (g + 1) * group, :] = scores[
                g * group : (g + 1) * group, g * slots : (g + 1) * slots
            ]
    row = lax.broadcasted_iota(jnp.int32, (requests, requests), 0)
    lane = lax.broadcasted_iota(jnp.int32, (requests, requests), 1)
    limits = jnp.where(row == lane, lengths_ref[...].astype(jnp.float32), 0.0)
    limits = jnp.broadcast_to(jnp.sum(limits, axis=1, keepdims=True), (requests, slots))
    slot = lax.broadcasted_iota(jnp.int32, (heads, slots), 1).astype(jnp.float32)
    for r in range(requests):
        rows = slice(r * heads, (r + 1) * heads)
        query = query_ref[rows, :]
        new_key = jnp.concatenate(
            [
                jnp.broadcast_to(key_ref[r * kv_heads + g : r * kv_heads + g + 1, :], (group, head))
                for g in range(kv_heads)
            ],
            axis=0,
        )
        new_score = jnp.sum(query * new_key, axis=1, keepdims=True) * inv_sqrt
        scores = jnp.where(slot < limits[r : r + 1, :], score_ref[rows, :] * inv_sqrt, -jnp.inf)
        row_max = jnp.maximum(jnp.max(scores, axis=1, keepdims=True), new_score)
        weights = jnp.exp(scores - row_max)
        new_weight = jnp.exp(new_score - row_max)
        total = jnp.sum(weights, axis=1, keepdims=True) + new_weight
        weight_ref[rows, :] = weights / total
        new_weight_ref[rows, :] = jnp.broadcast_to(new_weight / total, (heads, head))
    for r in range(requests):
        rows = slice(r * heads, (r + 1) * heads)
        zero = jnp.zeros((group, slots), jnp.float32)
        spread = jnp.concatenate(
            [
                jnp.concatenate(
                    [
                        weight_ref[r * heads + g * group : r * heads + (g + 1) * group, :]
                        if o == g
                        else zero
                        for o in range(kv_heads)
                    ],
                    axis=1,
                )
                for g in range(kv_heads)
            ],
            axis=0,
        ).astype(jnp.bfloat16)
        mixed = jnp.dot(
            spread,
            values_ref[r].reshape(kv_heads * slots, head),
            preferred_element_type=jnp.float32,
        )
        new_value = jnp.concatenate(
            [
                jnp.broadcast_to(
                    value_ref[r * kv_heads + g : r * kv_heads + g + 1, :], (group, head)
                )
                for g in range(kv_heads)
            ],
            axis=0,
        )
        new_weight = new_weight_ref[rows, :].astype(jnp.bfloat16).astype(jnp.float32)
        score_ref[rows, :] = mixed + new_weight * new_value
    for h in range(heads):
        out_ref[:, h * head : (h + 1) * head] = score_ref[
            pl.ds(h, requests, stride=heads), :
        ].astype(jnp.bfloat16)


def load_kernel(*refs):
    count = (len(refs) - 1) // 2
    sems = refs[-1]
    copies = [
        pltpu.make_async_copy(refs[i], refs[count + i], sems.at[i]) for i in range(count)
    ]
    for copy in copies:
        copy.start()
    for copy in copies:
        copy.wait()


def load(arrays):
    return pl.pallas_call(
        load_kernel,
        out_shape=[pltpu.VMEM(a.shape, a.dtype) for a in arrays],
        in_specs=[pl.BlockSpec(memory_space=pltpu.HBM)] * len(arrays),
        out_specs=[in_vmem()] * len(arrays),
        scratch_shapes=[pltpu.SemaphoreType.DMA((len(arrays),))],
        compiler_params=pltpu.CompilerParams(vmem_limit_bytes=LOAD_BYTES),
        cost_estimate=pl.CostEstimate(
            flops=0, bytes_accessed=sum(a.size for a in arrays) * 4, transcendentals=0
        ),
        name="load",
    )(*arrays)


def in_vmem():
    return pl.BlockSpec(memory_space=pltpu.VMEM)


def call(kernel, name, out_shape, scratch, arrays):
    return pl.pallas_call(
        kernel,
        out_shape=out_shape,
        in_specs=[in_vmem()] * len(arrays),
        out_specs=[in_vmem()] * len(out_shape),
        scratch_shapes=scratch,
        compiler_params=pltpu.CompilerParams(vmem_limit_bytes=VMEM_BYTES),
        name=name,
    )(*arrays)


def step(value, axis, size, k):
    return lax.ppermute(value, axis, [(i, i ^ k) for i in range(size)])


def exchange(value, axis, size):
    return [value] + [step(value, axis, size, k) for k in range(size - 1, 0, -1)]


def few_body(
    hidden,
    base_queries,
    base_keys,
    base_values,
    adapter_down_weight,
    adapter_up_query,
    adapter_up_key_value,
    cached_keys,
    cached_values,
    request_adapter,
    lengths,
):
    planes, columns = lax.axis_size("adapter"), lax.axis_size("tensor")
    requests = hidden.shape[0]
    every = requests * planes
    rank3 = adapter_down_weight.shape[1]
    head = cached_keys.shape[3]
    kv_heads = cached_keys.shape[1]
    heads = base_queries.shape[1] // head

    f32, bf16 = jnp.float32, jnp.bfloat16
    message = pack(request_adapter, hidden)
    mirror = step(message, "adapter", planes, planes - 1)
    near = step(message, "adapter", planes, 1)
    everyone = [message, mirror, step(mirror, "adapter", planes, 1), near]
    sent = [
        [
            (
                a * columns + t,
                plane_of(t % 2, (t // 2) ^ k ^ flip_of(a, t % 2)) * columns + a,
            )
            for a in range(planes)
            for t in range(columns)
        ]
        for k in range(2)
    ]
    other_query = step(adapter_up_query, "tensor", columns, 1)
    other_key_value = step(adapter_up_key_value, "tensor", columns, 1)
    (
        adapter_down_weight,
        adapter_up_query,
        adapter_up_key_value,
        base_queries,
        base_keys,
        base_values,
        cached_keys,
        cached_values,
    ) = load(
        [
            adapter_down_weight,
            adapter_up_query,
            adapter_up_key_value,
            base_queries,
            base_keys,
            base_values,
            cached_keys,
            cached_values,
        ]
    )
    partial, every_id = call(
        down_kernel,
        "down",
        [jax.ShapeDtypeStruct((rank3, every), f32), jax.ShapeDtypeStruct((every, LANES), f32)],
        [pltpu.VMEM((every, hidden.shape[1] + LANES), bf16)],
        [*everyone, adapter_down_weight],
    )
    summed = functools.reduce(jnp.add, exchange(partial, "tensor", columns)).astype(bf16)
    shrink = exchange(summed, "adapter", planes)
    width = 2 * adapter_up_query.shape[2] + 4 * adapter_up_key_value.shape[3]
    terms = call(
        up_kernel,
        "up",
        [jax.ShapeDtypeStruct((requests, width + LANES), f32)] * 2,
        [pltpu.VMEM((every, LANES), f32), pltpu.VMEM((every // 2, width), f32)],
        [
            every_id,
            *shrink,
            adapter_up_query,
            other_query,
            adapter_up_key_value,
            other_key_value,
        ],
    )
    arrived = [
        lax.ppermute(term.astype(jnp.float16), ("adapter", "tensor"), sent[k]).astype(f32)
        for k, term in enumerate(terms)
    ]
    cosine, sine = rotation_factors(lengths, head)
    return tuple(
        call(
            attend_kernel,
            "attend",
            [
                jax.ShapeDtypeStruct(base_queries.shape, bf16),
                jax.ShapeDtypeStruct(base_keys.shape, bf16),
                jax.ShapeDtypeStruct(base_values.shape, bf16),
            ],
            [
                pltpu.VMEM((2, requests, width), f32),
                pltpu.VMEM((requests * heads, head), f32),
                pltpu.VMEM((requests * kv_heads, head), f32),
                pltpu.VMEM((requests * kv_heads, head), f32),
                pltpu.VMEM((requests * heads, head), f32),
                pltpu.VMEM((requests * heads, head), f32),
                pltpu.VMEM((requests * heads, head), f32),
            ],
            [
                *arrived,
                base_queries,
                base_keys,
                base_values,
                lengths[None, :],
                cosine,
                sine,
                cached_keys,
                cached_values,
            ],
        )
    )


def rotate_pairs(vectors, positions):
    half_dim = vectors.shape[-1] // 2
    inv_freq = jnp.exp(
        -jnp.arange(half_dim, dtype=jnp.float32) * (2.0 / vectors.shape[-1]) * math.log(ROPE_BASE)
    )
    angles = positions.astype(jnp.float32)[:, None, None] * inv_freq[None, None, :]
    cosine = jnp.cos(angles)
    sine_part = jnp.sin(angles)
    front_half = vectors[..., :half_dim]
    back_half = vectors[..., half_dim:]
    return jnp.concatenate(
        [front_half * cosine - back_half * sine_part, front_half * sine_part + back_half * cosine],
        axis=-1,
    )


def attend_cache(query_vector, key_new, value_new, cached_keys, cached_values, lengths):
    local_requests, query_heads, head_dim = query_vector.shape
    kv_heads = key_new.shape[1]
    grouped = query_vector.reshape(local_requests, kv_heads, query_heads // kv_heads, head_dim)
    inv_sqrt = 1.0 / math.sqrt(head_dim)
    cache_scores = (
        jnp.einsum("rkge,rkpe->rkgp", grouped, cached_keys, preferred_element_type=jnp.float32)
        * inv_sqrt
    )
    in_cache = jnp.arange(cached_keys.shape[2], dtype=jnp.int32)[None, :] < lengths[:, None]
    cache_scores = jnp.where(in_cache[:, None, None, :], cache_scores, -jnp.inf)
    new_score = (
        jnp.einsum("rkge,rke->rkg", grouped, key_new, preferred_element_type=jnp.float32) * inv_sqrt
    )
    row_max = jnp.maximum(jnp.max(cache_scores, axis=-1), new_score)
    cache_weights = jnp.exp(cache_scores - row_max[..., None])
    new_weight = jnp.exp(new_score - row_max)
    softmax_sum = jnp.sum(cache_weights, axis=-1) + new_weight
    cache_weights = (cache_weights / softmax_sum[..., None]).astype(jnp.bfloat16)
    new_weight = (new_weight / softmax_sum).astype(jnp.bfloat16)
    mixed = jnp.einsum(
        "rkgp,rkpe->rkge", cache_weights, cached_values, preferred_element_type=jnp.float32
    )
    mixed = (
        mixed
        + new_weight.astype(jnp.float32)[..., None] * value_new.astype(jnp.float32)[:, :, None, :]
    )
    return mixed.reshape(local_requests, query_heads * head_dim).astype(jnp.bfloat16)


def many_body(
    hidden,
    base_queries,
    base_keys,
    base_values,
    adapter_down_weight,
    adapter_up_query,
    adapter_up_key_value,
    cached_keys,
    cached_values,
    request_adapter,
    lengths,
):
    owner_index = lax.axis_index("adapter")
    owning_requests = lax.axis_size("adapter")
    holding_count = adapter_down_weight.shape[0]
    rank_width = adapter_up_query.shape[1]
    local_requests = hidden.shape[0]
    everyone, every_id = (
        lax.all_gather(hidden, "adapter", axis=0, tiled=True),
        lax.all_gather(request_adapter, "adapter", axis=0, tiled=True),
    )
    every_row = everyone.shape[0]
    slot_of = every_id - owner_index * holding_count
    picked = slot_of[:, None] == jnp.arange(holding_count, dtype=jnp.int32)[None, :]
    picked_float = picked.astype(jnp.float32)
    flattened_lowered = adapter_down_weight.reshape(
        holding_count * 3 * rank_width, adapter_down_weight.shape[2]
    )
    partial_value = lax.dot_general(
        everyone, flattened_lowered, (((1,), (1,)), ((), ())), preferred_element_type=jnp.float32
    )
    summed = lax.psum(partial_value, "tensor")
    mine = jnp.sum(
        summed.reshape(every_row, holding_count, 3 * rank_width) * picked_float[:, :, None], axis=1
    )
    shrink_rank = lax.psum(mine.astype(jnp.bfloat16), "adapter").astype(jnp.float32)
    shrink_rank = shrink_rank.astype(jnp.bfloat16)

    def expand_rank(segment, factors):
        rows_used = jnp.take(factors, every_id, axis=0)
        rank_product = jnp.einsum(
            "rj,rjc->rc", segment, rows_used, preferred_element_type=jnp.float32
        )
        column_width = rank_product.shape[1]
        return (ADAPTER_SCALE * rank_product).reshape(
            owning_requests, every_row // owning_requests, 1, column_width
        )

    query_portion = expand_rank(shrink_rank[:, :rank_width], adapter_up_query)
    key_portion = expand_rank(
        shrink_rank[:, rank_width : 2 * rank_width], adapter_up_key_value[:, 0]
    )
    value_portion = expand_rank(shrink_rank[:, 2 * rank_width :], adapter_up_key_value[:, 1])
    arrived = (
        lax.all_to_all(
            lax.all_to_all(query_portion, "adapter", split_axis=0, concat_axis=2, tiled=True),
            "tensor",
            split_axis=2,
            concat_axis=0,
            tiled=True,
        ),
        lax.all_to_all(
            lax.all_to_all(key_portion, "adapter", split_axis=0, concat_axis=2, tiled=True),
            "tensor",
            split_axis=2,
            concat_axis=0,
            tiled=True,
        ),
        lax.all_to_all(
            lax.all_to_all(value_portion, "adapter", split_axis=0, concat_axis=2, tiled=True),
            "tensor",
            split_axis=2,
            concat_axis=0,
            tiled=True,
        ),
    )

    def columns(values):
        return jnp.transpose(values, (1, 2, 0, 3)).reshape(local_requests, -1)

    query_update = columns(arrived[0])
    key_update = columns(arrived[1])
    value_update = columns(arrived[2])
    head_dim = cached_keys.shape[3]
    kv_heads = cached_keys.shape[1]
    query_heads = base_queries.shape[1] // head_dim
    query_vector = rotate_pairs(
        (base_queries.astype(jnp.float32) + query_update).reshape(
            local_requests, query_heads, head_dim
        ),
        lengths,
    ).astype(jnp.bfloat16)
    fresh_keys = rotate_pairs(
        (base_keys.astype(jnp.float32) + key_update).reshape(local_requests, kv_heads, head_dim),
        lengths,
    ).astype(jnp.bfloat16)
    fresh_values = (base_values.astype(jnp.float32) + value_update).astype(jnp.bfloat16)
    attention = attend_cache(
        query_vector,
        fresh_keys,
        fresh_values.reshape(local_requests, kv_heads, head_dim),
        cached_keys,
        cached_values,
        lengths,
    )
    return (attention, fresh_keys.reshape(local_requests, kv_heads * head_dim), fresh_values)


def solution(mesh):
    few = mesh.shape["adapter"] == 4 and mesh.shape["tensor"] == 4
    return jax.shard_map(
        few_body if few else many_body,
        mesh=mesh,
        in_specs=(
            P(("groups", "adapter"), "tensor"),
            P(("groups", "adapter"), "tensor"),
            P(("groups", "adapter"), "tensor"),
            P(("groups", "adapter"), "tensor"),
            P("adapter", None, "tensor"),
            P(None, None, ("adapter", "tensor")),
            P(None, None, None, ("adapter", "tensor")),
            P(("groups", "adapter"), "tensor", None, None),
            P(("groups", "adapter"), "tensor", None, None),
            P(("groups", "adapter")),
            P(("groups", "adapter")),
        ),
        out_specs=(
            P(("groups", "adapter"), "tensor"),
            P(("groups", "adapter"), "tensor"),
            P(("groups", "adapter"), "tensor"),
        ),
        check_vma=False,
    )
```

```python
import functools
import math

import jax
import jax.numpy as jnp
from jax import lax
from jax.experimental import pallas as pl
from jax.experimental.pallas import tpu as pltpu
from jax.sharding import PartitionSpec as P

ADAPTER_SCALE = 0.5
ROPE_BASE = 500000.0
LANES = 128
VMEM_BYTES = 16 * 1024 * 1024
LOAD_BYTES = 52 * 1024 * 1024
PACK_BYTES = 60 * 1024 * 1024


def rotation_factors(positions, head_dim):
    half_dim = head_dim // 2
    inv_freq = jnp.exp(
        -jnp.arange(half_dim, dtype=jnp.float32) * (2.0 / head_dim) * math.log(ROPE_BASE)
    )
    angles = positions.astype(jnp.float32)[:, None] * inv_freq[None, :]
    return jnp.cos(angles), jnp.sin(angles)


FLIPS = 0b1111


def position():
    column = lax.axis_index("tensor")
    return lax.axis_index("adapter"), column % 2, column // 2


def plane_of(core, index):
    return (3 * index) ^ core


def core_of(plane):
    return (plane ^ (plane >> 1)) & 1


def index_of(plane):
    return plane >> 1


def flip_of(plane, core):
    return (FLIPS >> (2 * plane + core)) & 1


def pack_kernel(ids_in, hidden_in, out_ref, ids_ref, sems):
    requests, width = hidden_in.shape
    ids_copy = pltpu.make_async_copy(ids_in, ids_ref, sems.at[0])
    hidden_copy = pltpu.make_async_copy(hidden_in, out_ref.at[:, pl.ds(0, width)], sems.at[1])
    hidden_copy.start()
    ids_copy.start()
    ids_copy.wait()
    row = lax.broadcasted_iota(jnp.int32, (requests, LANES), 0)
    ids = jnp.zeros((requests, LANES), jnp.int32)
    for r in range(requests):
        ids = jnp.where(row == r, ids_ref[r], ids)
    out_ref[:, width:] = ids.astype(jnp.float32).astype(jnp.bfloat16)
    hidden_copy.wait()


def pack(request_adapter, hidden):
    requests, width = hidden.shape
    return pl.pallas_call(
        pack_kernel,
        out_shape=pltpu.VMEM((requests, width + LANES), jnp.bfloat16),
        in_specs=[pl.BlockSpec(memory_space=pltpu.HBM)] * 2,
        out_specs=in_vmem(),
        scratch_shapes=[
            pltpu.SMEM(request_adapter.shape, jnp.int32),
            pltpu.SemaphoreType.DMA((2,)),
        ],
        compiler_params=pltpu.CompilerParams(vmem_limit_bytes=PACK_BYTES),
        name="pack",
    )(request_adapter, hidden)


def down_kernel(*refs):
    *message_refs, down_ref, out_ref, ids_ref, rows_ref = refs
    place = position()[0]
    held, rank, width = down_ref.shape
    block = message_refs[0].shape[0]
    for k, message_ref in zip((0, 3, 2, 1), message_refs):
        start = pl.multiple_of((place ^ k) * block, block)
        rows_ref[pl.ds(start, block), :] = message_ref[...]
    ids = rows_ref[:, width:].astype(jnp.float32)
    ids_ref[...] = ids
    slot = jnp.transpose(ids)[0:1] - (place * held).astype(jnp.float32)
    product = lax.dot_general(
        down_ref[...].reshape(held * rank, width),
        rows_ref[:, :width],
        (((1,), (1,)), ((), ())),
        preferred_element_type=jnp.float32,
    )
    total = jnp.zeros(out_ref.shape, jnp.float32)
    for s in range(held):
        total += jnp.where(slot == s, product[s * rank : (s + 1) * rank], 0.0)
    out_ref[...] = total


def up_kernel(ids_ref, *refs):
    shrink_refs, query_refs, kv_refs = refs[:4], refs[4:6], refs[6:8]
    *out_refs, rows_ref, terms_ref = refs[8:]
    place, core, side = position()
    side ^= flip_of(place, core)
    shrink = shrink_refs[0][...].astype(jnp.float32)
    for ref in shrink_refs[1:]:
        shrink += ref[...].astype(jnp.float32)
    rank = shrink.shape[0] // 3
    every = shrink.shape[1]
    shrink = jnp.concatenate([shrink, jnp.zeros((LANES - 3 * rank, every), jnp.float32)], axis=0)
    rows_ref[...] = jnp.transpose(shrink)
    rows = every // 2
    block = out_refs[0].shape[0]
    starts = [pl.multiple_of(plane_of(core, i) * block, block) for i in range(2)]
    shrink = jnp.concatenate([rows_ref[pl.ds(start, block), :] for start in starts], axis=0)
    ids = jnp.concatenate([ids_ref[pl.ds(start, block), :] for start in starts], axis=0)
    lane = lax.broadcasted_iota(jnp.int32, (rows, LANES), 1)
    count = query_refs[0].shape[0]

    each = LANES // rank
    here = [ids - c * each == (lane // rank).astype(jnp.float32) for c in range(count // each)]

    def spread(part):
        part = jnp.concatenate([part] * each, axis=1)
        return jnp.concatenate(
            [jnp.where(mask, part, 0.0).astype(jnp.bfloat16) for mask in here], axis=1
        )

    query, key, value = [spread(shrink[:, i * rank : (i + 1) * rank]) for i in range(3)]
    width = query_refs[0].shape[2]
    half = kv_refs[0].shape[3]

    def product(rows_spread, factors):
        return ADAPTER_SCALE * jnp.dot(
            rows_spread,
            factors.reshape(count * rank, factors.shape[-1]),
            preferred_element_type=jnp.float32,
        )

    keys, new_values = [], []
    for which in range(2):
        column = pl.multiple_of((core ^ which) * width, width)
        terms_ref[:, pl.ds(column, width)] = product(query, query_refs[which][...])
        keys.append(product(key, kv_refs[which][:, 0]))
        new_values.append(product(value, kv_refs[which][:, 1]))
    for i, parts in enumerate((keys, new_values)):
        both = jnp.concatenate(parts, axis=1)
        both = jnp.where(core == 0, both, pltpu.roll(both, half, 1))
        terms_ref[:, 2 * width + i * LANES : 2 * width + (i + 1) * LANES] = both
    terms = terms_ref[...]
    largest = jnp.max(jnp.abs(terms), axis=1, keepdims=True)
    power = jnp.clip(jnp.ceil(jnp.log2(jnp.maximum(largest, 1e-30))), -100.0, 100.0)
    terms_ref[...] = terms * jnp.exp2(-power)
    total = terms.shape[1]
    for k, out_ref in enumerate(out_refs):
        at = pl.multiple_of((side ^ k) * block, block)
        out_ref[:, :total] = terms_ref[pl.ds(at, block), :]
        out_ref[:, total:] = jnp.broadcast_to(
            jnp.where((side ^ k) == 0, power[:block], power[block:]), (block, LANES)
        )


def attend_kernel(message, *refs):
    (
        term_ref,
        base_query_ref,
        base_key_ref,
        base_value_ref,
        lengths_ref,
        cosine_ref,
        sine_ref,
        keys_ref,
        values_ref,
    ) = refs[:9]
    (
        out_ref,
        fresh_key_ref,
        fresh_value_ref,
        mixed_ref,
        fresh_ref,
        query_ref,
        score_ref,
        weight_ref,
        new_weight_ref,
        sems,
    ) = refs[-10:]
    place, core, side = position()
    g = index_of(place) ^ flip_of(2 * side + core, core_of(place)) ^ message
    requests = base_query_ref.shape[0]
    slots, head = keys_ref.shape[2], keys_ref.shape[3]
    wide = base_query_ref.shape[1] // keys_ref.shape[1]
    group = wide // head
    half = head // 2
    total = term_ref.shape[1] - LANES
    scale = jnp.exp2(term_ref[:, total : total + 1])
    cosine, sine = cosine_ref[...], sine_ref[...]
    cosine = jnp.concatenate([cosine, cosine], axis=1)
    sine = jnp.concatenate([-sine, sine], axis=1)

    def rotate(u):
        return (u * cosine + pltpu.roll(u, half, 1) * sine).astype(jnp.bfloat16)

    def columns(width):
        return pl.ds(pl.multiple_of(g * width, width), width)

    base = base_query_ref[:, columns(wide)].astype(jnp.float32)
    for h in range(group):
        c = h * head
        u = base[:, c : c + head] + term_ref[:, c : c + head] * scale
        query_ref[pl.ds(h, requests, stride=group), :] = rotate(u).astype(jnp.float32)
    u = base_key_ref[:, columns(head)].astype(jnp.float32)
    new_key = rotate(u + term_ref[:, wide : wide + head] * scale)
    u = base_value_ref[:, columns(head)].astype(jnp.float32)
    new_value = (u + term_ref[:, wide + head : wide + 2 * head] * scale).astype(jnp.bfloat16)
    fresh_ref[0] = new_key
    fresh_ref[1] = new_value
    fresh_copies = [
        pltpu.make_async_copy(fresh_ref.at[i], ref.at[:, columns(head)], sems.at[i])
        for i, ref in enumerate((fresh_key_ref, fresh_value_ref))
    ]
    for copy in fresh_copies:
        copy.start()
    new_key, new_value = new_key.astype(jnp.float32), new_value.astype(jnp.float32)

    inv_sqrt = 1.0 / math.sqrt(head)
    zero = jnp.zeros((group, head), jnp.float32)

    def four(ref, r):
        parts = [ref[(r + i) * group : (r + i + 1) * group, :] for i in range(4)]
        return jnp.concatenate(
            [
                jnp.concatenate([parts[i], zero] if i % 2 == 0 else [zero, parts[i]], axis=1)
                for i in range(4)
            ],
            axis=0,
        ).astype(jnp.bfloat16)

    for r in range(0, requests, 4):
        keys = [keys_ref[r + i, g] for i in range(4)]
        keys = jnp.concatenate(
            [jnp.concatenate(keys[:2], axis=1), jnp.concatenate(keys[2:], axis=1)], axis=0
        )
        scores = lax.dot_general(
            four(query_ref, r), keys, (((1,), (1,)), ((), ())), preferred_element_type=jnp.float32
        )
        for i in range(4):
            score_ref[(r + i) * group : (r + i + 1) * group, :] = scores[
                i * group : (i + 1) * group, (i // 2) * slots : (i // 2 + 1) * slots
            ]
    row = lax.broadcasted_iota(jnp.int32, (requests, requests), 0)
    lane = lax.broadcasted_iota(jnp.int32, (requests, requests), 1)
    limits = jnp.where(row == lane, lengths_ref[...].astype(jnp.float32), 0.0)
    limits = jnp.broadcast_to(jnp.sum(limits, axis=1, keepdims=True), (requests, slots))
    slot = lax.broadcasted_iota(jnp.int32, (group, slots), 1).astype(jnp.float32)
    for r in range(requests):
        rows = slice(r * group, (r + 1) * group)
        new_score = (
            jnp.sum(query_ref[rows, :] * new_key[r : r + 1], axis=1, keepdims=True) * inv_sqrt
        )
        scores = jnp.where(slot < limits[r : r + 1], score_ref[rows, :] * inv_sqrt, -jnp.inf)
        row_max = jnp.maximum(jnp.max(scores, axis=1, keepdims=True), new_score)
        weights = jnp.exp(scores - row_max)
        new_weight = jnp.exp(new_score - row_max)
        total = jnp.sum(weights, axis=1, keepdims=True) + new_weight
        weight_ref[rows, :] = weights / total
        new_weight_ref[rows, :] = jnp.broadcast_to(new_weight / total, (group, head))
    for r in range(0, requests, 4):
        values = [values_ref[r + i, g] for i in range(4)]
        values = jnp.concatenate(
            [jnp.concatenate([values[i], values[i + 2]], axis=1) for i in range(2)], axis=0
        )
        mixed = jnp.dot(four(weight_ref, r), values, preferred_element_type=jnp.float32)
        for i in range(4):
            rows = slice((r + i) * group, (r + i + 1) * group)
            new_weight = new_weight_ref[rows, :].astype(jnp.bfloat16).astype(jnp.float32)
            score_ref[rows, :] = (
                mixed[i * group : (i + 1) * group, (i // 2) * head : (i // 2 + 1) * head]
                + new_weight * new_value[r + i : r + i + 1]
            )
    for h in range(group):
        mixed_ref[:, h * head : (h + 1) * head] = score_ref[
            pl.ds(h, requests, stride=group), :
        ].astype(jnp.bfloat16)
    copy = pltpu.make_async_copy(mixed_ref, out_ref.at[:, columns(wide)], sems.at[2])
    copy.start()
    for fresh_copy in fresh_copies:
        fresh_copy.wait()
    copy.wait()


def attend(message, arrays, before):
    base_queries, base_keys, base_values = arrays[1:4]
    requests, head = base_queries.shape[0], arrays[-1].shape[3]
    kv_heads = arrays[-1].shape[1]
    wide = base_queries.shape[1] // kv_heads
    rows = requests * wide // head
    shapes = [
        jax.ShapeDtypeStruct(a.shape, a.dtype) for a in (base_queries, base_keys, base_values)
    ]
    in_hbm = pl.BlockSpec(memory_space=pltpu.HBM)
    return pl.pallas_call(
        functools.partial(attend_kernel, message),
        out_shape=shapes,
        in_specs=[in_vmem()] * len(arrays) + [in_hbm] * len(before),
        out_specs=[in_hbm] * 3,
        input_output_aliases={len(arrays) + i: i for i in range(len(before))},
        scratch_shapes=[
            pltpu.VMEM((requests, wide), jnp.bfloat16),
            pltpu.VMEM((2, requests, head), jnp.bfloat16),
            pltpu.VMEM((rows, head), jnp.float32),
            pltpu.VMEM((rows, head), jnp.float32),
            pltpu.VMEM((rows, head), jnp.float32),
            pltpu.VMEM((rows, head), jnp.float32),
            pltpu.SemaphoreType.DMA((3,)),
        ],
        compiler_params=pltpu.CompilerParams(vmem_limit_bytes=VMEM_BYTES),
        name="attend",
    )(*arrays, *before)


def load_kernel(*refs):
    count = (len(refs) - 1) // 2
    sems = refs[-1]
    copies = [
        pltpu.make_async_copy(refs[i], refs[count + i], sems.at[i]) for i in range(count)
    ]
    for copy in copies:
        copy.start()
    for copy in copies:
        copy.wait()


def load(arrays):
    return pl.pallas_call(
        load_kernel,
        out_shape=[pltpu.VMEM(a.shape, a.dtype) for a in arrays],
        in_specs=[pl.BlockSpec(memory_space=pltpu.HBM)] * len(arrays),
        out_specs=[in_vmem()] * len(arrays),
        scratch_shapes=[pltpu.SemaphoreType.DMA((len(arrays),))],
        compiler_params=pltpu.CompilerParams(vmem_limit_bytes=LOAD_BYTES),
        cost_estimate=pl.CostEstimate(
            flops=0, bytes_accessed=sum(a.size for a in arrays) * 4, transcendentals=0
        ),
        name="load",
    )(*arrays)


def in_vmem():
    return pl.BlockSpec(memory_space=pltpu.VMEM)


def call(kernel, name, out_shape, scratch, arrays):
    return pl.pallas_call(
        kernel,
        out_shape=out_shape,
        in_specs=[in_vmem()] * len(arrays),
        out_specs=[in_vmem()] * len(out_shape),
        scratch_shapes=scratch,
        compiler_params=pltpu.CompilerParams(vmem_limit_bytes=VMEM_BYTES),
        name=name,
    )(*arrays)


def step(value, axis, size, k):
    return lax.ppermute(value, axis, [(i, i ^ k) for i in range(size)])


def exchange(value, axis, size):
    return [value] + [step(value, axis, size, k) for k in range(size - 1, 0, -1)]


def few_body(
    hidden,
    base_queries,
    base_keys,
    base_values,
    adapter_down_weight,
    adapter_up_query,
    adapter_up_key_value,
    cached_keys,
    cached_values,
    request_adapter,
    lengths,
):
    planes, columns = lax.axis_size("adapter"), lax.axis_size("tensor")
    requests = hidden.shape[0]
    every = requests * planes
    rank3 = adapter_down_weight.shape[1]
    head = cached_keys.shape[3]
    kv_heads = cached_keys.shape[1]
    heads = base_queries.shape[1] // head

    f32, bf16 = jnp.float32, jnp.bfloat16
    message = pack(request_adapter, hidden)
    mirror = step(message, "adapter", planes, planes - 1)
    near = step(message, "adapter", planes, 1)
    everyone = [message, mirror, step(mirror, "adapter", planes, 1), near]
    sent = [
        [
            (
                a * columns + t,
                plane_of(t % 2, (t // 2) ^ k ^ flip_of(a, t % 2)) * columns + a,
            )
            for a in range(planes)
            for t in range(columns)
        ]
        for k in range(2)
    ]
    other_query = step(adapter_up_query, "tensor", columns, 1)
    other_key_value = step(adapter_up_key_value, "tensor", columns, 1)
    (
        adapter_down_weight,
        adapter_up_query,
        adapter_up_key_value,
        base_queries,
        base_keys,
        base_values,
        cached_keys,
        cached_values,
    ) = load(
        [
            adapter_down_weight,
            adapter_up_query,
            adapter_up_key_value,
            base_queries,
            base_keys,
            base_values,
            cached_keys,
            cached_values,
        ]
    )
    partial, every_id = call(
        down_kernel,
        "down",
        [jax.ShapeDtypeStruct((rank3, every), f32), jax.ShapeDtypeStruct((every, LANES), f32)],
        [pltpu.VMEM((every, hidden.shape[1] + LANES), bf16)],
        [*everyone, adapter_down_weight],
    )
    summed = functools.reduce(jnp.add, exchange(partial, "tensor", columns)).astype(bf16)
    shrink = exchange(summed, "adapter", planes)
    width = 2 * adapter_up_query.shape[2] + 4 * adapter_up_key_value.shape[3]
    terms = call(
        up_kernel,
        "up",
        [jax.ShapeDtypeStruct((requests, width + LANES), f32)] * 2,
        [pltpu.VMEM((every, LANES), f32), pltpu.VMEM((every // 2, width), f32)],
        [
            every_id,
            *shrink,
            adapter_up_query,
            other_query,
            adapter_up_key_value,
            other_key_value,
        ],
    )
    arrived = [
        lax.ppermute(term.astype(jnp.float16), ("adapter", "tensor"), sent[k]).astype(f32)
        for k, term in enumerate(terms)
    ]
    cosine, sine = rotation_factors(lengths, head)
    outs = []
    for k, term in enumerate(arrived):
        arrays = [
            term,
            base_queries,
            base_keys,
            base_values,
            lengths[None, :],
            cosine,
            sine,
            cached_keys,
            cached_values,
        ]
        outs = attend(k, arrays, outs)
    return tuple(outs)


def rotate_pairs(vectors, positions):
    half_dim = vectors.shape[-1] // 2
    inv_freq = jnp.exp(
        -jnp.arange(half_dim, dtype=jnp.float32) * (2.0 / vectors.shape[-1]) * math.log(ROPE_BASE)
    )
    angles = positions.astype(jnp.float32)[:, None, None] * inv_freq[None, None, :]
    cosine = jnp.cos(angles)
    sine_part = jnp.sin(angles)
    front_half = vectors[..., :half_dim]
    back_half = vectors[..., half_dim:]
    return jnp.concatenate(
        [front_half * cosine - back_half * sine_part, front_half * sine_part + back_half * cosine],
        axis=-1,
    )


def attend_cache(query_vector, key_new, value_new, cached_keys, cached_values, lengths):
    local_requests, query_heads, head_dim = query_vector.shape
    kv_heads = key_new.shape[1]
    grouped = query_vector.reshape(local_requests, kv_heads, query_heads // kv_heads, head_dim)
    inv_sqrt = 1.0 / math.sqrt(head_dim)
    cache_scores = (
        jnp.einsum("rkge,rkpe->rkgp", grouped, cached_keys, preferred_element_type=jnp.float32)
        * inv_sqrt
    )
    in_cache = jnp.arange(cached_keys.shape[2], dtype=jnp.int32)[None, :] < lengths[:, None]
    cache_scores = jnp.where(in_cache[:, None, None, :], cache_scores, -jnp.inf)
    new_score = (
        jnp.einsum("rkge,rke->rkg", grouped, key_new, preferred_element_type=jnp.float32) * inv_sqrt
    )
    row_max = jnp.maximum(jnp.max(cache_scores, axis=-1), new_score)
    cache_weights = jnp.exp(cache_scores - row_max[..., None])
    new_weight = jnp.exp(new_score - row_max)
    softmax_sum = jnp.sum(cache_weights, axis=-1) + new_weight
    cache_weights = (cache_weights / softmax_sum[..., None]).astype(jnp.bfloat16)
    new_weight = (new_weight / softmax_sum).astype(jnp.bfloat16)
    mixed = jnp.einsum(
        "rkgp,rkpe->rkge", cache_weights, cached_values, preferred_element_type=jnp.float32
    )
    mixed = (
        mixed
        + new_weight.astype(jnp.float32)[..., None] * value_new.astype(jnp.float32)[:, :, None, :]
    )
    return mixed.reshape(local_requests, query_heads * head_dim).astype(jnp.bfloat16)


def many_body(
    hidden,
    base_queries,
    base_keys,
    base_values,
    adapter_down_weight,
    adapter_up_query,
    adapter_up_key_value,
    cached_keys,
    cached_values,
    request_adapter,
    lengths,
):
    owner_index = lax.axis_index("adapter")
    owning_requests = lax.axis_size("adapter")
    holding_count = adapter_down_weight.shape[0]
    rank_width = adapter_up_query.shape[1]
    local_requests = hidden.shape[0]
    everyone, every_id = (
        lax.all_gather(hidden, "adapter", axis=0, tiled=True),
        lax.all_gather(request_adapter, "adapter", axis=0, tiled=True),
    )
    every_row = everyone.shape[0]
    slot_of = every_id - owner_index * holding_count
    picked = slot_of[:, None] == jnp.arange(holding_count, dtype=jnp.int32)[None, :]
    picked_float = picked.astype(jnp.float32)
    flattened_lowered = adapter_down_weight.reshape(
        holding_count * 3 * rank_width, adapter_down_weight.shape[2]
    )
    partial_value = lax.dot_general(
        everyone, flattened_lowered, (((1,), (1,)), ((), ())), preferred_element_type=jnp.float32
    )
    summed = lax.psum(partial_value, "tensor")
    mine = jnp.sum(
        summed.reshape(every_row, holding_count, 3 * rank_width) * picked_float[:, :, None], axis=1
    )
    shrink_rank = lax.psum(mine.astype(jnp.bfloat16), "adapter").astype(jnp.float32)
    shrink_rank = shrink_rank.astype(jnp.bfloat16)

    def expand_rank(segment, factors):
        rows_used = jnp.take(factors, every_id, axis=0)
        rank_product = jnp.einsum(
            "rj,rjc->rc", segment, rows_used, preferred_element_type=jnp.float32
        )
        column_width = rank_product.shape[1]
        return (ADAPTER_SCALE * rank_product).reshape(
            owning_requests, every_row // owning_requests, 1, column_width
        )

    query_portion = expand_rank(shrink_rank[:, :rank_width], adapter_up_query)
    key_portion = expand_rank(
        shrink_rank[:, rank_width : 2 * rank_width], adapter_up_key_value[:, 0]
    )
    value_portion = expand_rank(shrink_rank[:, 2 * rank_width :], adapter_up_key_value[:, 1])
    arrived = (
        lax.all_to_all(
            lax.all_to_all(query_portion, "adapter", split_axis=0, concat_axis=2, tiled=True),
            "tensor",
            split_axis=2,
            concat_axis=0,
            tiled=True,
        ),
        lax.all_to_all(
            lax.all_to_all(key_portion, "adapter", split_axis=0, concat_axis=2, tiled=True),
            "tensor",
            split_axis=2,
            concat_axis=0,
            tiled=True,
        ),
        lax.all_to_all(
            lax.all_to_all(value_portion, "adapter", split_axis=0, concat_axis=2, tiled=True),
            "tensor",
            split_axis=2,
            concat_axis=0,
            tiled=True,
        ),
    )

    def columns(values):
        return jnp.transpose(values, (1, 2, 0, 3)).reshape(local_requests, -1)

    query_update = columns(arrived[0])
    key_update = columns(arrived[1])
    value_update = columns(arrived[2])
    head_dim = cached_keys.shape[3]
    kv_heads = cached_keys.shape[1]
    query_heads = base_queries.shape[1] // head_dim
    query_vector = rotate_pairs(
        (base_queries.astype(jnp.float32) + query_update).reshape(
            local_requests, query_heads, head_dim
        ),
        lengths,
    ).astype(jnp.bfloat16)
    fresh_keys = rotate_pairs(
        (base_keys.astype(jnp.float32) + key_update).reshape(local_requests, kv_heads, head_dim),
        lengths,
    ).astype(jnp.bfloat16)
    fresh_values = (base_values.astype(jnp.float32) + value_update).astype(jnp.bfloat16)
    attention = attend_cache(
        query_vector,
        fresh_keys,
        fresh_values.reshape(local_requests, kv_heads, head_dim),
        cached_keys,
        cached_values,
        lengths,
    )
    return (attention, fresh_keys.reshape(local_requests, kv_heads * head_dim), fresh_values)


def solution(mesh):
    few = mesh.shape["adapter"] == 4 and mesh.shape["tensor"] == 4
    return jax.shard_map(
        few_body if few else many_body,
        mesh=mesh,
        in_specs=(
            P(("groups", "adapter"), "tensor"),
            P(("groups", "adapter"), "tensor"),
            P(("groups", "adapter"), "tensor"),
            P(("groups", "adapter"), "tensor"),
            P("adapter", None, "tensor"),
            P(None, None, ("adapter", "tensor")),
            P(None, None, None, ("adapter", "tensor")),
            P(("groups", "adapter"), "tensor", None, None),
            P(("groups", "adapter"), "tensor", None, None),
            P(("groups", "adapter")),
            P(("groups", "adapter")),
        ),
        out_specs=(
            P(("groups", "adapter"), "tensor"),
            P(("groups", "adapter"), "tensor"),
            P(("groups", "adapter"), "tensor"),
        ),
        check_vma=False,
    )
```

```python
import functools
import math

import jax
import jax.numpy as jnp
from jax import lax
from jax.experimental import pallas as pl
from jax.experimental.pallas import tpu as pltpu
from jax.sharding import PartitionSpec as P

ADAPTER_SCALE = 0.5
ROPE_BASE = 500000.0
LANES = 128
VMEM_BYTES = 16 * 1024 * 1024
LOAD_BYTES = 52 * 1024 * 1024
PACK_BYTES = 60 * 1024 * 1024


def rotation_factors(positions, head_dim):
    half_dim = head_dim // 2
    inv_freq = jnp.exp(
        -jnp.arange(half_dim, dtype=jnp.float32) * (2.0 / head_dim) * math.log(ROPE_BASE)
    )
    angles = positions.astype(jnp.float32)[:, None] * inv_freq[None, :]
    return jnp.cos(angles), jnp.sin(angles)


ORDER = (((2, 3), (1, 0)), ((1, 2), (3, 0)), ((0, 1), (2, 3)), ((1, 3), (2, 0)))
PLANES = [
    sum(ORDER[a][c][i] << (4 * a + 2 * i) for a in range(4) for i in range(2)) for c in range(2)
]
INDEX = sum(i << (4 * a + ORDER[a][c][i]) for a in range(4) for c in range(2) for i in range(2))


def position():
    column = lax.axis_index("tensor")
    return lax.axis_index("adapter"), column % 2, column // 2


def plane_of(place, core, index):
    both = jnp.where(core == 0, PLANES[0], PLANES[1])
    return (both >> (4 * place + 2 * index)) & 3


def index_of(plane, place):
    return (INDEX >> (4 * plane + place)) & 1


def pack_kernel(ids_in, hidden_in, out_ref, ids_ref, sems):
    requests, width = hidden_in.shape
    ids_copy = pltpu.make_async_copy(ids_in, ids_ref, sems.at[0])
    hidden_copy = pltpu.make_async_copy(hidden_in, out_ref.at[:, pl.ds(0, width)], sems.at[1])
    hidden_copy.start()
    ids_copy.start()
    ids_copy.wait()
    row = lax.broadcasted_iota(jnp.int32, (requests, LANES), 0)
    ids = jnp.zeros((requests, LANES), jnp.int32)
    for r in range(requests):
        ids = jnp.where(row == r, ids_ref[r], ids)
    out_ref[:, width:] = ids.astype(jnp.float32).astype(jnp.bfloat16)
    hidden_copy.wait()


def pack(request_adapter, hidden):
    requests, width = hidden.shape
    return pl.pallas_call(
        pack_kernel,
        out_shape=pltpu.VMEM((requests, width + LANES), jnp.bfloat16),
        in_specs=[pl.BlockSpec(memory_space=pltpu.HBM)] * 2,
        out_specs=in_vmem(),
        scratch_shapes=[
            pltpu.SMEM(request_adapter.shape, jnp.int32),
            pltpu.SemaphoreType.DMA((2,)),
        ],
        compiler_params=pltpu.CompilerParams(vmem_limit_bytes=PACK_BYTES),
        name="pack",
    )(request_adapter, hidden)


def down_kernel(*refs):
    *message_refs, down_ref, out_ref, ids_ref, rows_ref = refs
    place = position()[0]
    held, rank, width = down_ref.shape
    block = message_refs[0].shape[0]
    for k, message_ref in zip((0, 3, 2, 1), message_refs):
        start = pl.multiple_of((place ^ k) * block, block)
        rows_ref[pl.ds(start, block), :] = message_ref[...]
    ids = rows_ref[:, width:].astype(jnp.float32)
    ids_ref[...] = ids
    slot = jnp.transpose(ids)[0:1] - (place * held).astype(jnp.float32)
    product = lax.dot_general(
        down_ref[...].reshape(held * rank, width),
        rows_ref[:, :width],
        (((1,), (1,)), ((), ())),
        preferred_element_type=jnp.float32,
    )
    total = jnp.zeros(out_ref.shape, jnp.float32)
    for s in range(held):
        total += jnp.where(slot == s, product[s * rank : (s + 1) * rank], 0.0)
    out_ref[...] = total


def up_kernel(ids_ref, *refs):
    shrink_refs, query_refs, kv_refs = refs[:4], refs[4:6], refs[6:8]
    *out_refs, rows_ref, terms_ref = refs[8:]
    place, core, side = position()
    shrink = shrink_refs[0][...].astype(jnp.float32)
    for ref in shrink_refs[1:]:
        shrink += ref[...].astype(jnp.float32)
    rank = shrink.shape[0] // 3
    every = shrink.shape[1]
    shrink = jnp.concatenate([shrink, jnp.zeros((LANES - 3 * rank, every), jnp.float32)], axis=0)
    rows_ref[...] = jnp.transpose(shrink)
    rows = every // 2
    block = out_refs[0].shape[0]
    starts = [pl.multiple_of(plane_of(place, core, i) * block, block) for i in range(2)]
    shrink = jnp.concatenate([rows_ref[pl.ds(start, block), :] for start in starts], axis=0)
    ids = jnp.concatenate([ids_ref[pl.ds(start, block), :] for start in starts], axis=0)
    lane = lax.broadcasted_iota(jnp.int32, (rows, LANES), 1)
    count = query_refs[0].shape[0]

    each = LANES // rank
    here = [ids - c * each == (lane // rank).astype(jnp.float32) for c in range(count // each)]

    def spread(part):
        part = jnp.concatenate([part] * each, axis=1)
        return jnp.concatenate(
            [jnp.where(mask, part, 0.0).astype(jnp.bfloat16) for mask in here], axis=1
        )

    query, key, value = [spread(shrink[:, i * rank : (i + 1) * rank]) for i in range(3)]
    width = query_refs[0].shape[2]
    half = kv_refs[0].shape[3]

    def product(rows_spread, factors):
        return ADAPTER_SCALE * jnp.dot(
            rows_spread,
            factors.reshape(count * rank, factors.shape[-1]),
            preferred_element_type=jnp.float32,
        )

    keys, new_values = [], []
    for which in range(2):
        column = pl.multiple_of((core ^ which) * width, width)
        terms_ref[:, pl.ds(column, width)] = product(query, query_refs[which][...])
        keys.append(product(key, kv_refs[which][:, 0]))
        new_values.append(product(value, kv_refs[which][:, 1]))
    for i, parts in enumerate((keys, new_values)):
        both = jnp.concatenate(parts, axis=1)
        both = jnp.where(core == 0, both, pltpu.roll(both, half, 1))
        terms_ref[:, 2 * width + i * LANES : 2 * width + (i + 1) * LANES] = both
    terms = terms_ref[...]
    largest = jnp.max(jnp.abs(terms), axis=1, keepdims=True)
    power = jnp.clip(jnp.ceil(jnp.log2(jnp.maximum(largest, 1e-30))), -100.0, 100.0)
    terms_ref[...] = terms * jnp.exp2(-power)
    total = terms.shape[1]
    for k, out_ref in enumerate(out_refs):
        at = pl.multiple_of((side ^ k) * block, block)
        out_ref[:, :total] = terms_ref[pl.ds(at, block), :]
        out_ref[:, total:] = jnp.broadcast_to(
            jnp.where((side ^ k) == 0, power[:block], power[block:]), (block, LANES)
        )


def attend_kernel(message, *refs):
    (
        term_ref,
        base_query_ref,
        base_key_ref,
        base_value_ref,
        lengths_ref,
        cosine_ref,
        sine_ref,
        keys_ref,
        values_ref,
    ) = refs[:9]
    (
        out_ref,
        fresh_key_ref,
        fresh_value_ref,
        mixed_ref,
        fresh_ref,
        query_ref,
        score_ref,
        weight_ref,
        new_weight_ref,
        sems,
    ) = refs[-10:]
    place, core, side = position()
    g = index_of(2 * side + core, place) ^ message
    requests = base_query_ref.shape[0]
    slots, head = keys_ref.shape[2], keys_ref.shape[3]
    wide = base_query_ref.shape[1] // keys_ref.shape[1]
    group = wide // head
    half = head // 2
    total = term_ref.shape[1] - LANES
    scale = jnp.exp2(term_ref[:, total : total + 1])
    cosine, sine = cosine_ref[...], sine_ref[...]
    cosine = jnp.concatenate([cosine, cosine], axis=1)
    sine = jnp.concatenate([-sine, sine], axis=1)

    def rotate(u):
        return (u * cosine + pltpu.roll(u, half, 1) * sine).astype(jnp.bfloat16)

    def columns(width):
        return pl.ds(pl.multiple_of(g * width, width), width)

    base = base_query_ref[:, columns(wide)].astype(jnp.float32)
    for h in range(group):
        c = h * head
        u = base[:, c : c + head] + term_ref[:, c : c + head] * scale
        query_ref[pl.ds(h, requests, stride=group), :] = rotate(u).astype(jnp.float32)
    u = base_key_ref[:, columns(head)].astype(jnp.float32)
    new_key = rotate(u + term_ref[:, wide : wide + head] * scale)
    u = base_value_ref[:, columns(head)].astype(jnp.float32)
    new_value = (u + term_ref[:, wide + head : wide + 2 * head] * scale).astype(jnp.bfloat16)
    fresh_ref[0] = new_key
    fresh_ref[1] = new_value
    fresh_copies = [
        pltpu.make_async_copy(fresh_ref.at[i], ref.at[:, columns(head)], sems.at[i])
        for i, ref in enumerate((fresh_key_ref, fresh_value_ref))
    ]
    for copy in fresh_copies:
        copy.start()
    new_key, new_value = new_key.astype(jnp.float32), new_value.astype(jnp.float32)

    inv_sqrt = 1.0 / math.sqrt(head)
    zero = jnp.zeros((group, head), jnp.float32)

    def four(ref, r):
        parts = [ref[(r + i) * group : (r + i + 1) * group, :] for i in range(4)]
        return jnp.concatenate(
            [
                jnp.concatenate([parts[i], zero] if i % 2 == 0 else [zero, parts[i]], axis=1)
                for i in range(4)
            ],
            axis=0,
        ).astype(jnp.bfloat16)

    for r in range(0, requests, 4):
        keys = [keys_ref[r + i, g] for i in range(4)]
        keys = jnp.concatenate(
            [jnp.concatenate(keys[:2], axis=1), jnp.concatenate(keys[2:], axis=1)], axis=0
        )
        scores = lax.dot_general(
            four(query_ref, r), keys, (((1,), (1,)), ((), ())), preferred_element_type=jnp.float32
        )
        for i in range(4):
            score_ref[(r + i) * group : (r + i + 1) * group, :] = scores[
                i * group : (i + 1) * group, (i // 2) * slots : (i // 2 + 1) * slots
            ]
    row = lax.broadcasted_iota(jnp.int32, (requests, requests), 0)
    lane = lax.broadcasted_iota(jnp.int32, (requests, requests), 1)
    limits = jnp.where(row == lane, lengths_ref[...].astype(jnp.float32), 0.0)
    limits = jnp.broadcast_to(jnp.sum(limits, axis=1, keepdims=True), (requests, slots))
    slot = lax.broadcasted_iota(jnp.int32, (group, slots), 1).astype(jnp.float32)
    for r in range(requests):
        rows = slice(r * group, (r + 1) * group)
        new_score = (
            jnp.sum(query_ref[rows, :] * new_key[r : r + 1], axis=1, keepdims=True) * inv_sqrt
        )
        scores = jnp.where(slot < limits[r : r + 1], score_ref[rows, :] * inv_sqrt, -jnp.inf)
        row_max = jnp.maximum(jnp.max(scores, axis=1, keepdims=True), new_score)
        weights = jnp.exp(scores - row_max)
        new_weight = jnp.exp(new_score - row_max)
        total = jnp.sum(weights, axis=1, keepdims=True) + new_weight
        weight_ref[rows, :] = weights / total
        new_weight_ref[rows, :] = jnp.broadcast_to(new_weight / total, (group, head))
    for r in range(0, requests, 4):
        values = [values_ref[r + i, g] for i in range(4)]
        values = jnp.concatenate(
            [jnp.concatenate([values[i], values[i + 2]], axis=1) for i in range(2)], axis=0
        )
        mixed = jnp.dot(four(weight_ref, r), values, preferred_element_type=jnp.float32)
        for i in range(4):
            rows = slice((r + i) * group, (r + i + 1) * group)
            new_weight = new_weight_ref[rows, :].astype(jnp.bfloat16).astype(jnp.float32)
            score_ref[rows, :] = (
                mixed[i * group : (i + 1) * group, (i // 2) * head : (i // 2 + 1) * head]
                + new_weight * new_value[r + i : r + i + 1]
            )
    for h in range(group):
        mixed_ref[:, h * head : (h + 1) * head] = score_ref[
            pl.ds(h, requests, stride=group), :
        ].astype(jnp.bfloat16)
    copy = pltpu.make_async_copy(mixed_ref, out_ref.at[:, columns(wide)], sems.at[2])
    copy.start()
    for fresh_copy in fresh_copies:
        fresh_copy.wait()
    copy.wait()


def attend(message, arrays, before):
    base_queries, base_keys, base_values = arrays[1:4]
    requests, head = base_queries.shape[0], arrays[-1].shape[3]
    kv_heads = arrays[-1].shape[1]
    wide = base_queries.shape[1] // kv_heads
    rows = requests * wide // head
    shapes = [
        jax.ShapeDtypeStruct(a.shape, a.dtype) for a in (base_queries, base_keys, base_values)
    ]
    in_hbm = pl.BlockSpec(memory_space=pltpu.HBM)
    return pl.pallas_call(
        functools.partial(attend_kernel, message),
        out_shape=shapes,
        in_specs=[in_vmem()] * len(arrays) + [in_hbm] * len(before),
        out_specs=[in_hbm] * 3,
        input_output_aliases={len(arrays) + i: i for i in range(len(before))},
        scratch_shapes=[
            pltpu.VMEM((requests, wide), jnp.bfloat16),
            pltpu.VMEM((2, requests, head), jnp.bfloat16),
            pltpu.VMEM((rows, head), jnp.float32),
            pltpu.VMEM((rows, head), jnp.float32),
            pltpu.VMEM((rows, head), jnp.float32),
            pltpu.VMEM((rows, head), jnp.float32),
            pltpu.SemaphoreType.DMA((3,)),
        ],
        compiler_params=pltpu.CompilerParams(vmem_limit_bytes=VMEM_BYTES),
        name="attend",
    )(*arrays, *before)


def load_kernel(*refs):
    count = (len(refs) - 1) // 2
    sems = refs[-1]
    copies = [
        pltpu.make_async_copy(refs[i], refs[count + i], sems.at[i]) for i in range(count)
    ]
    for copy in copies:
        copy.start()
    for copy in copies:
        copy.wait()


def load(arrays):
    return pl.pallas_call(
        load_kernel,
        out_shape=[pltpu.VMEM(a.shape, a.dtype) for a in arrays],
        in_specs=[pl.BlockSpec(memory_space=pltpu.HBM)] * len(arrays),
        out_specs=[in_vmem()] * len(arrays),
        scratch_shapes=[pltpu.SemaphoreType.DMA((len(arrays),))],
        compiler_params=pltpu.CompilerParams(vmem_limit_bytes=LOAD_BYTES),
        cost_estimate=pl.CostEstimate(
            flops=0, bytes_accessed=sum(a.size for a in arrays) * 4, transcendentals=0
        ),
        name="load",
    )(*arrays)


def in_vmem():
    return pl.BlockSpec(memory_space=pltpu.VMEM)


def call(kernel, name, out_shape, scratch, arrays):
    return pl.pallas_call(
        kernel,
        out_shape=out_shape,
        in_specs=[in_vmem()] * len(arrays),
        out_specs=[in_vmem()] * len(out_shape),
        scratch_shapes=scratch,
        compiler_params=pltpu.CompilerParams(vmem_limit_bytes=VMEM_BYTES),
        name=name,
    )(*arrays)


def step(value, axis, size, k):
    return lax.ppermute(value, axis, [(i, i ^ k) for i in range(size)])


def exchange(value, axis, size):
    return [value] + [step(value, axis, size, k) for k in range(size - 1, 0, -1)]


def few_body(
    hidden,
    base_queries,
    base_keys,
    base_values,
    adapter_down_weight,
    adapter_up_query,
    adapter_up_key_value,
    cached_keys,
    cached_values,
    request_adapter,
    lengths,
):
    planes, columns = lax.axis_size("adapter"), lax.axis_size("tensor")
    requests = hidden.shape[0]
    every = requests * planes
    rank3 = adapter_down_weight.shape[1]
    head = cached_keys.shape[3]
    kv_heads = cached_keys.shape[1]
    heads = base_queries.shape[1] // head

    f32, bf16 = jnp.float32, jnp.bfloat16
    message = pack(request_adapter, hidden)
    mirror = step(message, "adapter", planes, planes - 1)
    near = step(message, "adapter", planes, 1)
    everyone = [message, mirror, step(mirror, "adapter", planes, 1), near]
    sent = [
        [
            (a * columns + t, ORDER[a][t % 2][(t // 2) ^ k] * columns + a)
            for a in range(planes)
            for t in range(columns)
        ]
        for k in range(2)
    ]
    other_query = step(adapter_up_query, "tensor", columns, 1)
    other_key_value = step(adapter_up_key_value, "tensor", columns, 1)
    (
        adapter_down_weight,
        adapter_up_query,
        adapter_up_key_value,
        base_queries,
        base_keys,
        base_values,
        cached_keys,
        cached_values,
    ) = load(
        [
            adapter_down_weight,
            adapter_up_query,
            adapter_up_key_value,
            base_queries,
            base_keys,
            base_values,
            cached_keys,
            cached_values,
        ]
    )
    partial, every_id = call(
        down_kernel,
        "down",
        [jax.ShapeDtypeStruct((rank3, every), f32), jax.ShapeDtypeStruct((every, LANES), f32)],
        [pltpu.VMEM((every, hidden.shape[1] + LANES), bf16)],
        [*everyone, adapter_down_weight],
    )
    summed = functools.reduce(jnp.add, exchange(partial, "tensor", columns)).astype(bf16)
    shrink = exchange(summed, "adapter", planes)
    width = 2 * adapter_up_query.shape[2] + 4 * adapter_up_key_value.shape[3]
    terms = call(
        up_kernel,
        "up",
        [jax.ShapeDtypeStruct((requests, width + LANES), f32)] * 2,
        [pltpu.VMEM((every, LANES), f32), pltpu.VMEM((every // 2, width), f32)],
        [
            every_id,
            *shrink,
            adapter_up_query,
            other_query,
            adapter_up_key_value,
            other_key_value,
        ],
    )
    arrived = [
        lax.ppermute(term.astype(jnp.float16), ("adapter", "tensor"), sent[k]).astype(f32)
        for k, term in enumerate(terms)
    ]
    cosine, sine = rotation_factors(lengths, head)
    outs = []
    for k, term in enumerate(arrived):
        arrays = [
            term,
            base_queries,
            base_keys,
            base_values,
            lengths[None, :],
            cosine,
            sine,
            cached_keys,
            cached_values,
        ]
        outs = attend(k, arrays, outs)
    return tuple(outs)


def rotate_pairs(vectors, positions):
    half_dim = vectors.shape[-1] // 2
    inv_freq = jnp.exp(
        -jnp.arange(half_dim, dtype=jnp.float32) * (2.0 / vectors.shape[-1]) * math.log(ROPE_BASE)
    )
    angles = positions.astype(jnp.float32)[:, None, None] * inv_freq[None, None, :]
    cosine = jnp.cos(angles)
    sine_part = jnp.sin(angles)
    front_half = vectors[..., :half_dim]
    back_half = vectors[..., half_dim:]
    return jnp.concatenate(
        [front_half * cosine - back_half * sine_part, front_half * sine_part + back_half * cosine],
        axis=-1,
    )


def attend_cache(query_vector, key_new, value_new, cached_keys, cached_values, lengths):
    local_requests, query_heads, head_dim = query_vector.shape
    kv_heads = key_new.shape[1]
    grouped = query_vector.reshape(local_requests, kv_heads, query_heads // kv_heads, head_dim)
    inv_sqrt = 1.0 / math.sqrt(head_dim)
    cache_scores = (
        jnp.einsum("rkge,rkpe->rkgp", grouped, cached_keys, preferred_element_type=jnp.float32)
        * inv_sqrt
    )
    in_cache = jnp.arange(cached_keys.shape[2], dtype=jnp.int32)[None, :] < lengths[:, None]
    cache_scores = jnp.where(in_cache[:, None, None, :], cache_scores, -jnp.inf)
    new_score = (
        jnp.einsum("rkge,rke->rkg", grouped, key_new, preferred_element_type=jnp.float32) * inv_sqrt
    )
    row_max = jnp.maximum(jnp.max(cache_scores, axis=-1), new_score)
    cache_weights = jnp.exp(cache_scores - row_max[..., None])
    new_weight = jnp.exp(new_score - row_max)
    softmax_sum = jnp.sum(cache_weights, axis=-1) + new_weight
    cache_weights = (cache_weights / softmax_sum[..., None]).astype(jnp.bfloat16)
    new_weight = (new_weight / softmax_sum).astype(jnp.bfloat16)
    mixed = jnp.einsum(
        "rkgp,rkpe->rkge", cache_weights, cached_values, preferred_element_type=jnp.float32
    )
    mixed = (
        mixed
        + new_weight.astype(jnp.float32)[..., None] * value_new.astype(jnp.float32)[:, :, None, :]
    )
    return mixed.reshape(local_requests, query_heads * head_dim).astype(jnp.bfloat16)


def many_body(
    hidden,
    base_queries,
    base_keys,
    base_values,
    adapter_down_weight,
    adapter_up_query,
    adapter_up_key_value,
    cached_keys,
    cached_values,
    request_adapter,
    lengths,
):
    owner_index = lax.axis_index("adapter")
    owning_requests = lax.axis_size("adapter")
    holding_count = adapter_down_weight.shape[0]
    rank_width = adapter_up_query.shape[1]
    local_requests = hidden.shape[0]
    everyone, every_id = (
        lax.all_gather(hidden, "adapter", axis=0, tiled=True),
        lax.all_gather(request_adapter, "adapter", axis=0, tiled=True),
    )
    every_row = everyone.shape[0]
    slot_of = every_id - owner_index * holding_count
    picked = slot_of[:, None] == jnp.arange(holding_count, dtype=jnp.int32)[None, :]
    picked_float = picked.astype(jnp.float32)
    flattened_lowered = adapter_down_weight.reshape(
        holding_count * 3 * rank_width, adapter_down_weight.shape[2]
    )
    partial_value = lax.dot_general(
        everyone, flattened_lowered, (((1,), (1,)), ((), ())), preferred_element_type=jnp.float32
    )
    summed = lax.psum(partial_value, "tensor")
    mine = jnp.sum(
        summed.reshape(every_row, holding_count, 3 * rank_width) * picked_float[:, :, None], axis=1
    )
    shrink_rank = lax.psum(mine.astype(jnp.bfloat16), "adapter").astype(jnp.float32)
    shrink_rank = shrink_rank.astype(jnp.bfloat16)

    def expand_rank(segment, factors):
        rows_used = jnp.take(factors, every_id, axis=0)
        rank_product = jnp.einsum(
            "rj,rjc->rc", segment, rows_used, preferred_element_type=jnp.float32
        )
        column_width = rank_product.shape[1]
        return (ADAPTER_SCALE * rank_product).reshape(
            owning_requests, every_row // owning_requests, 1, column_width
        )

    query_portion = expand_rank(shrink_rank[:, :rank_width], adapter_up_query)
    key_portion = expand_rank(
        shrink_rank[:, rank_width : 2 * rank_width], adapter_up_key_value[:, 0]
    )
    value_portion = expand_rank(shrink_rank[:, 2 * rank_width :], adapter_up_key_value[:, 1])
    arrived = (
        lax.all_to_all(
            lax.all_to_all(query_portion, "adapter", split_axis=0, concat_axis=2, tiled=True),
            "tensor",
            split_axis=2,
            concat_axis=0,
            tiled=True,
        ),
        lax.all_to_all(
            lax.all_to_all(key_portion, "adapter", split_axis=0, concat_axis=2, tiled=True),
            "tensor",
            split_axis=2,
            concat_axis=0,
            tiled=True,
        ),
        lax.all_to_all(
            lax.all_to_all(value_portion, "adapter", split_axis=0, concat_axis=2, tiled=True),
            "tensor",
            split_axis=2,
            concat_axis=0,
            tiled=True,
        ),
    )

    def columns(values):
        return jnp.transpose(values, (1, 2, 0, 3)).reshape(local_requests, -1)

    query_update = columns(arrived[0])
    key_update = columns(arrived[1])
    value_update = columns(arrived[2])
    head_dim = cached_keys.shape[3]
    kv_heads = cached_keys.shape[1]
    query_heads = base_queries.shape[1] // head_dim
    query_vector = rotate_pairs(
        (base_queries.astype(jnp.float32) + query_update).reshape(
            local_requests, query_heads, head_dim
        ),
        lengths,
    ).astype(jnp.bfloat16)
    fresh_keys = rotate_pairs(
        (base_keys.astype(jnp.float32) + key_update).reshape(local_requests, kv_heads, head_dim),
        lengths,
    ).astype(jnp.bfloat16)
    fresh_values = (base_values.astype(jnp.float32) + value_update).astype(jnp.bfloat16)
    attention = attend_cache(
        query_vector,
        fresh_keys,
        fresh_values.reshape(local_requests, kv_heads, head_dim),
        cached_keys,
        cached_values,
        lengths,
    )
    return (attention, fresh_keys.reshape(local_requests, kv_heads * head_dim), fresh_values)


def solution(mesh):
    few = mesh.shape["adapter"] == 4 and mesh.shape["tensor"] == 4
    return jax.shard_map(
        few_body if few else many_body,
        mesh=mesh,
        in_specs=(
            P(("groups", "adapter"), "tensor"),
            P(("groups", "adapter"), "tensor"),
            P(("groups", "adapter"), "tensor"),
            P(("groups", "adapter"), "tensor"),
            P("adapter", None, "tensor"),
            P(None, None, ("adapter", "tensor")),
            P(None, None, None, ("adapter", "tensor")),
            P(("groups", "adapter"), "tensor", None, None),
            P(("groups", "adapter"), "tensor", None, None),
            P(("groups", "adapter")),
            P(("groups", "adapter")),
        ),
        out_specs=(
            P(("groups", "adapter"), "tensor"),
            P(("groups", "adapter"), "tensor"),
            P(("groups", "adapter"), "tensor"),
        ),
        check_vma=False,
    )
```

```python
import functools
import math

import jax
import jax.numpy as jnp
from jax import lax
from jax.experimental import pallas as pl
from jax.experimental.pallas import tpu as pltpu
from jax.sharding import PartitionSpec as P

ADAPTER_SCALE = 0.5
ROPE_BASE = 500000.0
LANES = 128
VMEM_BYTES = 16 * 1024 * 1024
LOAD_BYTES = 52 * 1024 * 1024
PACK_BYTES = 60 * 1024 * 1024


def rotation_factors(positions, head_dim):
    half_dim = head_dim // 2
    inv_freq = jnp.exp(
        -jnp.arange(half_dim, dtype=jnp.float32) * (2.0 / head_dim) * math.log(ROPE_BASE)
    )
    angles = positions.astype(jnp.float32)[:, None] * inv_freq[None, :]
    return jnp.cos(angles), jnp.sin(angles)


ORDER = (((2, 1), (3, 0)), ((1, 2), (3, 0)), ((1, 0), (2, 3)), ((0, 3), (1, 2)))
PLANES = [
    sum(ORDER[a][c][i] << (4 * a + 2 * i) for a in range(4) for i in range(2)) for c in range(2)
]
INDEX = sum(i << (4 * a + ORDER[a][c][i]) for a in range(4) for c in range(2) for i in range(2))


def position():
    column = lax.axis_index("tensor")
    return lax.axis_index("adapter"), column % 2, column // 2


def plane_of(place, core, index):
    both = jnp.where(core == 0, PLANES[0], PLANES[1])
    return (both >> (4 * place + 2 * index)) & 3


def index_of(plane, place):
    return (INDEX >> (4 * plane + place)) & 1


def pack_kernel(ids_in, hidden_in, out_ref, ids_ref, sems):
    requests, width = hidden_in.shape
    ids_copy = pltpu.make_async_copy(ids_in, ids_ref, sems.at[0])
    hidden_copy = pltpu.make_async_copy(hidden_in, out_ref.at[:, pl.ds(0, width)], sems.at[1])
    hidden_copy.start()
    ids_copy.start()
    ids_copy.wait()
    row = lax.broadcasted_iota(jnp.int32, (requests, LANES), 0)
    ids = jnp.zeros((requests, LANES), jnp.int32)
    for r in range(requests):
        ids = jnp.where(row == r, ids_ref[r], ids)
    out_ref[:, width:] = ids.astype(jnp.float32).astype(jnp.bfloat16)
    hidden_copy.wait()


def pack(request_adapter, hidden):
    requests, width = hidden.shape
    return pl.pallas_call(
        pack_kernel,
        out_shape=pltpu.VMEM((requests, width + LANES), jnp.bfloat16),
        in_specs=[pl.BlockSpec(memory_space=pltpu.HBM)] * 2,
        out_specs=in_vmem(),
        scratch_shapes=[
            pltpu.SMEM(request_adapter.shape, jnp.int32),
            pltpu.SemaphoreType.DMA((2,)),
        ],
        compiler_params=pltpu.CompilerParams(vmem_limit_bytes=PACK_BYTES),
        name="pack",
    )(request_adapter, hidden)


def down_kernel(*refs):
    *message_refs, down_ref, out_ref, ids_ref, rows_ref = refs
    place = position()[0]
    held, rank, width = down_ref.shape
    block = message_refs[0].shape[0]
    for k, message_ref in zip((0, 3, 2, 1), message_refs):
        start = pl.multiple_of((place ^ k) * block, block)
        rows_ref[pl.ds(start, block), :] = message_ref[...]
    ids = rows_ref[:, width:].astype(jnp.float32)
    ids_ref[...] = ids
    slot = jnp.transpose(ids)[0:1] - (place * held).astype(jnp.float32)
    product = lax.dot_general(
        down_ref[...].reshape(held * rank, width),
        rows_ref[:, :width],
        (((1,), (1,)), ((), ())),
        preferred_element_type=jnp.float32,
    )
    total = jnp.zeros(out_ref.shape, jnp.float32)
    for s in range(held):
        total += jnp.where(slot == s, product[s * rank : (s + 1) * rank], 0.0)
    out_ref[...] = total


def up_kernel(ids_ref, *refs):
    shrink_refs, query_refs, kv_refs = refs[:4], refs[4:6], refs[6:8]
    *out_refs, rows_ref, terms_ref = refs[8:]
    place, core, side = position()
    shrink = shrink_refs[0][...].astype(jnp.float32)
    for ref in shrink_refs[1:]:
        shrink += ref[...].astype(jnp.float32)
    rank = shrink.shape[0] // 3
    every = shrink.shape[1]
    shrink = jnp.concatenate([shrink, jnp.zeros((LANES - 3 * rank, every), jnp.float32)], axis=0)
    rows_ref[...] = jnp.transpose(shrink)
    rows = every // 2
    block = out_refs[0].shape[0]
    starts = [pl.multiple_of(plane_of(place, core, i) * block, block) for i in range(2)]
    shrink = jnp.concatenate([rows_ref[pl.ds(start, block), :] for start in starts], axis=0)
    ids = jnp.concatenate([ids_ref[pl.ds(start, block), :] for start in starts], axis=0)
    lane = lax.broadcasted_iota(jnp.int32, (rows, LANES), 1)
    count = query_refs[0].shape[0]

    each = LANES // rank
    here = [ids - c * each == (lane // rank).astype(jnp.float32) for c in range(count // each)]

    def spread(part):
        part = jnp.concatenate([part] * each, axis=1)
        return jnp.concatenate(
            [jnp.where(mask, part, 0.0).astype(jnp.bfloat16) for mask in here], axis=1
        )

    query, key, value = [spread(shrink[:, i * rank : (i + 1) * rank]) for i in range(3)]
    width = query_refs[0].shape[2]
    half = kv_refs[0].shape[3]

    def product(rows_spread, factors):
        return ADAPTER_SCALE * jnp.dot(
            rows_spread,
            factors.reshape(count * rank, factors.shape[-1]),
            preferred_element_type=jnp.float32,
        )

    keys, new_values = [], []
    for which in range(2):
        column = pl.multiple_of((core ^ which) * width, width)
        terms_ref[:, pl.ds(column, width)] = product(query, query_refs[which][...])
        keys.append(product(key, kv_refs[which][:, 0]))
        new_values.append(product(value, kv_refs[which][:, 1]))
    for i, parts in enumerate((keys, new_values)):
        both = jnp.concatenate(parts, axis=1)
        both = jnp.where(core == 0, both, pltpu.roll(both, half, 1))
        terms_ref[:, 2 * width + i * LANES : 2 * width + (i + 1) * LANES] = both
    terms = terms_ref[...]
    largest = jnp.max(jnp.abs(terms), axis=1, keepdims=True)
    power = jnp.clip(jnp.ceil(jnp.log2(jnp.maximum(largest, 1e-30))), -100.0, 100.0)
    terms_ref[...] = terms * jnp.exp2(-power)
    total = terms.shape[1]
    for k, out_ref in enumerate(out_refs):
        at = pl.multiple_of((side ^ k) * block, block)
        out_ref[:, :total] = terms_ref[pl.ds(at, block), :]
        out_ref[:, total:] = jnp.broadcast_to(
            jnp.where((side ^ k) == 0, power[:block], power[block:]), (block, LANES)
        )


def attend_kernel(message, *refs):
    (
        term_ref,
        base_query_ref,
        base_key_ref,
        base_value_ref,
        lengths_ref,
        cosine_ref,
        sine_ref,
        keys_ref,
        values_ref,
    ) = refs[:9]
    (
        out_ref,
        fresh_key_ref,
        fresh_value_ref,
        mixed_ref,
        fresh_ref,
        query_ref,
        score_ref,
        weight_ref,
        new_weight_ref,
        sems,
    ) = refs[-10:]
    place, core, side = position()
    g = index_of(2 * side + core, place) ^ message
    requests = base_query_ref.shape[0]
    slots, head = keys_ref.shape[2], keys_ref.shape[3]
    wide = base_query_ref.shape[1] // keys_ref.shape[1]
    group = wide // head
    half = head // 2
    total = term_ref.shape[1] - LANES
    scale = jnp.exp2(term_ref[:, total : total + 1])
    cosine, sine = cosine_ref[...], sine_ref[...]
    cosine = jnp.concatenate([cosine, cosine], axis=1)
    sine = jnp.concatenate([-sine, sine], axis=1)

    def rotate(u):
        return (u * cosine + pltpu.roll(u, half, 1) * sine).astype(jnp.bfloat16)

    def columns(width):
        return pl.ds(pl.multiple_of(g * width, width), width)

    base = base_query_ref[:, columns(wide)].astype(jnp.float32)
    for h in range(group):
        c = h * head
        u = base[:, c : c + head] + term_ref[:, c : c + head] * scale
        query_ref[pl.ds(h, requests, stride=group), :] = rotate(u).astype(jnp.float32)
    u = base_key_ref[:, columns(head)].astype(jnp.float32)
    new_key = rotate(u + term_ref[:, wide : wide + head] * scale)
    u = base_value_ref[:, columns(head)].astype(jnp.float32)
    new_value = (u + term_ref[:, wide + head : wide + 2 * head] * scale).astype(jnp.bfloat16)
    fresh_ref[0] = new_key
    fresh_ref[1] = new_value
    fresh_copies = [
        pltpu.make_async_copy(fresh_ref.at[i], ref.at[:, columns(head)], sems.at[i])
        for i, ref in enumerate((fresh_key_ref, fresh_value_ref))
    ]
    for copy in fresh_copies:
        copy.start()
    new_key, new_value = new_key.astype(jnp.float32), new_value.astype(jnp.float32)

    inv_sqrt = 1.0 / math.sqrt(head)
    zero = jnp.zeros((group, head), jnp.float32)

    def four(ref, r):
        parts = [ref[(r + i) * group : (r + i + 1) * group, :] for i in range(4)]
        return jnp.concatenate(
            [
                jnp.concatenate([parts[i], zero] if i % 2 == 0 else [zero, parts[i]], axis=1)
                for i in range(4)
            ],
            axis=0,
        ).astype(jnp.bfloat16)

    for r in range(0, requests, 4):
        keys = [keys_ref[r + i, g] for i in range(4)]
        keys = jnp.concatenate(
            [jnp.concatenate(keys[:2], axis=1), jnp.concatenate(keys[2:], axis=1)], axis=0
        )
        scores = lax.dot_general(
            four(query_ref, r), keys, (((1,), (1,)), ((), ())), preferred_element_type=jnp.float32
        )
        for i in range(4):
            score_ref[(r + i) * group : (r + i + 1) * group, :] = scores[
                i * group : (i + 1) * group, (i // 2) * slots : (i // 2 + 1) * slots
            ]
    row = lax.broadcasted_iota(jnp.int32, (requests, requests), 0)
    lane = lax.broadcasted_iota(jnp.int32, (requests, requests), 1)
    limits = jnp.where(row == lane, lengths_ref[...].astype(jnp.float32), 0.0)
    limits = jnp.broadcast_to(jnp.sum(limits, axis=1, keepdims=True), (requests, slots))
    slot = lax.broadcasted_iota(jnp.int32, (group, slots), 1).astype(jnp.float32)
    for r in range(requests):
        rows = slice(r * group, (r + 1) * group)
        new_score = (
            jnp.sum(query_ref[rows, :] * new_key[r : r + 1], axis=1, keepdims=True) * inv_sqrt
        )
        scores = jnp.where(slot < limits[r : r + 1], score_ref[rows, :] * inv_sqrt, -jnp.inf)
        row_max = jnp.maximum(jnp.max(scores, axis=1, keepdims=True), new_score)
        weights = jnp.exp(scores - row_max)
        new_weight = jnp.exp(new_score - row_max)
        total = jnp.sum(weights, axis=1, keepdims=True) + new_weight
        weight_ref[rows, :] = weights / total
        new_weight_ref[rows, :] = jnp.broadcast_to(new_weight / total, (group, head))
    for r in range(0, requests, 4):
        values = [values_ref[r + i, g] for i in range(4)]
        values = jnp.concatenate(
            [jnp.concatenate([values[i], values[i + 2]], axis=1) for i in range(2)], axis=0
        )
        mixed = jnp.dot(four(weight_ref, r), values, preferred_element_type=jnp.float32)
        for i in range(4):
            rows = slice((r + i) * group, (r + i + 1) * group)
            new_weight = new_weight_ref[rows, :].astype(jnp.bfloat16).astype(jnp.float32)
            score_ref[rows, :] = (
                mixed[i * group : (i + 1) * group, (i // 2) * head : (i // 2 + 1) * head]
                + new_weight * new_value[r + i : r + i + 1]
            )
    for h in range(group):
        mixed_ref[:, h * head : (h + 1) * head] = score_ref[
            pl.ds(h, requests, stride=group), :
        ].astype(jnp.bfloat16)
    copy = pltpu.make_async_copy(mixed_ref, out_ref.at[:, columns(wide)], sems.at[2])
    copy.start()
    for fresh_copy in fresh_copies:
        fresh_copy.wait()
    copy.wait()


def attend(message, arrays, before):
    base_queries, base_keys, base_values = arrays[1:4]
    requests, head = base_queries.shape[0], arrays[-1].shape[3]
    kv_heads = arrays[-1].shape[1]
    wide = base_queries.shape[1] // kv_heads
    rows = requests * wide // head
    shapes = [
        jax.ShapeDtypeStruct(a.shape, a.dtype) for a in (base_queries, base_keys, base_values)
    ]
    in_hbm = pl.BlockSpec(memory_space=pltpu.HBM)
    return pl.pallas_call(
        functools.partial(attend_kernel, message),
        out_shape=shapes,
        in_specs=[in_vmem()] * len(arrays) + [in_hbm] * len(before),
        out_specs=[in_hbm] * 3,
        input_output_aliases={len(arrays) + i: i for i in range(len(before))},
        scratch_shapes=[
            pltpu.VMEM((requests, wide), jnp.bfloat16),
            pltpu.VMEM((2, requests, head), jnp.bfloat16),
            pltpu.VMEM((rows, head), jnp.float32),
            pltpu.VMEM((rows, head), jnp.float32),
            pltpu.VMEM((rows, head), jnp.float32),
            pltpu.VMEM((rows, head), jnp.float32),
            pltpu.SemaphoreType.DMA((3,)),
        ],
        compiler_params=pltpu.CompilerParams(vmem_limit_bytes=VMEM_BYTES),
        name="attend",
    )(*arrays, *before)


def load_kernel(*refs):
    count = (len(refs) - 1) // 2
    sems = refs[-1]
    copies = [
        pltpu.make_async_copy(refs[i], refs[count + i], sems.at[i]) for i in range(count)
    ]
    for copy in copies:
        copy.start()
    for copy in copies:
        copy.wait()


def load(arrays):
    return pl.pallas_call(
        load_kernel,
        out_shape=[pltpu.VMEM(a.shape, a.dtype) for a in arrays],
        in_specs=[pl.BlockSpec(memory_space=pltpu.HBM)] * len(arrays),
        out_specs=[in_vmem()] * len(arrays),
        scratch_shapes=[pltpu.SemaphoreType.DMA((len(arrays),))],
        compiler_params=pltpu.CompilerParams(vmem_limit_bytes=LOAD_BYTES),
        cost_estimate=pl.CostEstimate(
            flops=0, bytes_accessed=sum(a.size for a in arrays) * 4, transcendentals=0
        ),
        name="load",
    )(*arrays)


def in_vmem():
    return pl.BlockSpec(memory_space=pltpu.VMEM)


def call(kernel, name, out_shape, scratch, arrays):
    return pl.pallas_call(
        kernel,
        out_shape=out_shape,
        in_specs=[in_vmem()] * len(arrays),
        out_specs=[in_vmem()] * len(out_shape),
        scratch_shapes=scratch,
        compiler_params=pltpu.CompilerParams(vmem_limit_bytes=VMEM_BYTES),
        name=name,
    )(*arrays)


def step(value, axis, size, k):
    return lax.ppermute(value, axis, [(i, i ^ k) for i in range(size)])


def exchange(value, axis, size):
    return [value] + [step(value, axis, size, k) for k in range(size - 1, 0, -1)]


def few_body(
    hidden,
    base_queries,
    base_keys,
    base_values,
    adapter_down_weight,
    adapter_up_query,
    adapter_up_key_value,
    cached_keys,
    cached_values,
    request_adapter,
    lengths,
):
    planes, columns = lax.axis_size("adapter"), lax.axis_size("tensor")
    requests = hidden.shape[0]
    every = requests * planes
    rank3 = adapter_down_weight.shape[1]
    head = cached_keys.shape[3]
    kv_heads = cached_keys.shape[1]
    heads = base_queries.shape[1] // head

    f32, bf16 = jnp.float32, jnp.bfloat16
    message = pack(request_adapter, hidden)
    mirror = step(message, "adapter", planes, planes - 1)
    near = step(message, "adapter", planes, 1)
    everyone = [message, mirror, step(mirror, "adapter", planes, 1), near]
    sent = [
        [
            (a * columns + t, ORDER[a][t % 2][(t // 2) ^ k] * columns + a)
            for a in range(planes)
            for t in range(columns)
        ]
        for k in range(2)
    ]
    message, early_query = lax.optimization_barrier((message, adapter_up_query))
    everyone[0] = message
    other_query = step(early_query, "tensor", columns, 1)
    other_key_value = step(adapter_up_key_value, "tensor", columns, 1)
    (
        adapter_down_weight,
        adapter_up_query,
        adapter_up_key_value,
        base_queries,
        base_keys,
        base_values,
        cached_keys,
        cached_values,
    ) = load(
        [
            adapter_down_weight,
            adapter_up_query,
            adapter_up_key_value,
            base_queries,
            base_keys,
            base_values,
            cached_keys,
            cached_values,
        ]
    )
    partial, every_id = call(
        down_kernel,
        "down",
        [jax.ShapeDtypeStruct((rank3, every), f32), jax.ShapeDtypeStruct((every, LANES), f32)],
        [pltpu.VMEM((every, hidden.shape[1] + LANES), bf16)],
        [*everyone, adapter_down_weight],
    )
    summed = functools.reduce(jnp.add, exchange(partial, "tensor", columns)).astype(bf16)
    shrink = exchange(summed, "adapter", planes)
    width = 2 * adapter_up_query.shape[2] + 4 * adapter_up_key_value.shape[3]
    terms = call(
        up_kernel,
        "up",
        [jax.ShapeDtypeStruct((requests, width + LANES), f32)] * 2,
        [pltpu.VMEM((every, LANES), f32), pltpu.VMEM((every // 2, width), f32)],
        [
            every_id,
            *shrink,
            adapter_up_query,
            other_query,
            adapter_up_key_value,
            other_key_value,
        ],
    )
    arrived = [
        lax.ppermute(term.astype(jnp.float16), ("adapter", "tensor"), sent[k]).astype(f32)
        for k, term in enumerate(terms)
    ]
    cosine, sine = rotation_factors(lengths, head)
    outs = []
    for k, term in enumerate(arrived):
        arrays = [
            term,
            base_queries,
            base_keys,
            base_values,
            lengths[None, :],
            cosine,
            sine,
            cached_keys,
            cached_values,
        ]
        outs = attend(k, arrays, outs)
    return tuple(outs)


def rotate_pairs(vectors, positions):
    half_dim = vectors.shape[-1] // 2
    inv_freq = jnp.exp(
        -jnp.arange(half_dim, dtype=jnp.float32) * (2.0 / vectors.shape[-1]) * math.log(ROPE_BASE)
    )
    angles = positions.astype(jnp.float32)[:, None, None] * inv_freq[None, None, :]
    cosine = jnp.cos(angles)
    sine_part = jnp.sin(angles)
    front_half = vectors[..., :half_dim]
    back_half = vectors[..., half_dim:]
    return jnp.concatenate(
        [front_half * cosine - back_half * sine_part, front_half * sine_part + back_half * cosine],
        axis=-1,
    )


def attend_cache(query_vector, key_new, value_new, cached_keys, cached_values, lengths):
    local_requests, query_heads, head_dim = query_vector.shape
    kv_heads = key_new.shape[1]
    grouped = query_vector.reshape(local_requests, kv_heads, query_heads // kv_heads, head_dim)
    inv_sqrt = 1.0 / math.sqrt(head_dim)
    cache_scores = (
        jnp.einsum("rkge,rkpe->rkgp", grouped, cached_keys, preferred_element_type=jnp.float32)
        * inv_sqrt
    )
    in_cache = jnp.arange(cached_keys.shape[2], dtype=jnp.int32)[None, :] < lengths[:, None]
    cache_scores = jnp.where(in_cache[:, None, None, :], cache_scores, -jnp.inf)
    new_score = (
        jnp.einsum("rkge,rke->rkg", grouped, key_new, preferred_element_type=jnp.float32) * inv_sqrt
    )
    row_max = jnp.maximum(jnp.max(cache_scores, axis=-1), new_score)
    cache_weights = jnp.exp(cache_scores - row_max[..., None])
    new_weight = jnp.exp(new_score - row_max)
    softmax_sum = jnp.sum(cache_weights, axis=-1) + new_weight
    cache_weights = (cache_weights / softmax_sum[..., None]).astype(jnp.bfloat16)
    new_weight = (new_weight / softmax_sum).astype(jnp.bfloat16)
    mixed = jnp.einsum(
        "rkgp,rkpe->rkge", cache_weights, cached_values, preferred_element_type=jnp.float32
    )
    mixed = (
        mixed
        + new_weight.astype(jnp.float32)[..., None] * value_new.astype(jnp.float32)[:, :, None, :]
    )
    return mixed.reshape(local_requests, query_heads * head_dim).astype(jnp.bfloat16)


def many_body(
    hidden,
    base_queries,
    base_keys,
    base_values,
    adapter_down_weight,
    adapter_up_query,
    adapter_up_key_value,
    cached_keys,
    cached_values,
    request_adapter,
    lengths,
):
    owner_index = lax.axis_index("adapter")
    owning_requests = lax.axis_size("adapter")
    holding_count = adapter_down_weight.shape[0]
    rank_width = adapter_up_query.shape[1]
    local_requests = hidden.shape[0]
    everyone, every_id = (
        lax.all_gather(hidden, "adapter", axis=0, tiled=True),
        lax.all_gather(request_adapter, "adapter", axis=0, tiled=True),
    )
    every_row = everyone.shape[0]
    slot_of = every_id - owner_index * holding_count
    picked = slot_of[:, None] == jnp.arange(holding_count, dtype=jnp.int32)[None, :]
    picked_float = picked.astype(jnp.float32)
    flattened_lowered = adapter_down_weight.reshape(
        holding_count * 3 * rank_width, adapter_down_weight.shape[2]
    )
    partial_value = lax.dot_general(
        everyone, flattened_lowered, (((1,), (1,)), ((), ())), preferred_element_type=jnp.float32
    )
    summed = lax.psum(partial_value, "tensor")
    mine = jnp.sum(
        summed.reshape(every_row, holding_count, 3 * rank_width) * picked_float[:, :, None], axis=1
    )
    shrink_rank = lax.psum(mine.astype(jnp.bfloat16), "adapter").astype(jnp.float32)
    shrink_rank = shrink_rank.astype(jnp.bfloat16)

    def expand_rank(segment, factors):
        rows_used = jnp.take(factors, every_id, axis=0)
        rank_product = jnp.einsum(
            "rj,rjc->rc", segment, rows_used, preferred_element_type=jnp.float32
        )
        column_width = rank_product.shape[1]
        return (ADAPTER_SCALE * rank_product).reshape(
            owning_requests, every_row // owning_requests, 1, column_width
        )

    query_portion = expand_rank(shrink_rank[:, :rank_width], adapter_up_query)
    key_portion = expand_rank(
        shrink_rank[:, rank_width : 2 * rank_width], adapter_up_key_value[:, 0]
    )
    value_portion = expand_rank(shrink_rank[:, 2 * rank_width :], adapter_up_key_value[:, 1])
    arrived = (
        lax.all_to_all(
            lax.all_to_all(query_portion, "adapter", split_axis=0, concat_axis=2, tiled=True),
            "tensor",
            split_axis=2,
            concat_axis=0,
            tiled=True,
        ),
        lax.all_to_all(
            lax.all_to_all(key_portion, "adapter", split_axis=0, concat_axis=2, tiled=True),
            "tensor",
            split_axis=2,
            concat_axis=0,
            tiled=True,
        ),
        lax.all_to_all(
            lax.all_to_all(value_portion, "adapter", split_axis=0, concat_axis=2, tiled=True),
            "tensor",
            split_axis=2,
            concat_axis=0,
            tiled=True,
        ),
    )

    def columns(values):
        return jnp.transpose(values, (1, 2, 0, 3)).reshape(local_requests, -1)

    query_update = columns(arrived[0])
    key_update = columns(arrived[1])
    value_update = columns(arrived[2])
    head_dim = cached_keys.shape[3]
    kv_heads = cached_keys.shape[1]
    query_heads = base_queries.shape[1] // head_dim
    query_vector = rotate_pairs(
        (base_queries.astype(jnp.float32) + query_update).reshape(
            local_requests, query_heads, head_dim
        ),
        lengths,
    ).astype(jnp.bfloat16)
    fresh_keys = rotate_pairs(
        (base_keys.astype(jnp.float32) + key_update).reshape(local_requests, kv_heads, head_dim),
        lengths,
    ).astype(jnp.bfloat16)
    fresh_values = (base_values.astype(jnp.float32) + value_update).astype(jnp.bfloat16)
    attention = attend_cache(
        query_vector,
        fresh_keys,
        fresh_values.reshape(local_requests, kv_heads, head_dim),
        cached_keys,
        cached_values,
        lengths,
    )
    return (attention, fresh_keys.reshape(local_requests, kv_heads * head_dim), fresh_values)


def solution(mesh):
    few = mesh.shape["adapter"] == 4 and mesh.shape["tensor"] == 4
    return jax.shard_map(
        few_body if few else many_body,
        mesh=mesh,
        in_specs=(
            P(("groups", "adapter"), "tensor"),
            P(("groups", "adapter"), "tensor"),
            P(("groups", "adapter"), "tensor"),
            P(("groups", "adapter"), "tensor"),
            P("adapter", None, "tensor"),
            P(None, None, ("adapter", "tensor")),
            P(None, None, None, ("adapter", "tensor")),
            P(("groups", "adapter"), "tensor", None, None),
            P(("groups", "adapter"), "tensor", None, None),
            P(("groups", "adapter")),
            P(("groups", "adapter")),
        ),
        out_specs=(
            P(("groups", "adapter"), "tensor"),
            P(("groups", "adapter"), "tensor"),
            P(("groups", "adapter"), "tensor"),
        ),
        check_vma=False,
    )
```

```python
import functools
import math

import jax
import jax.numpy as jnp
from jax import lax
from jax.experimental import pallas as pl
from jax.experimental.pallas import tpu as pltpu
from jax.sharding import PartitionSpec as P

ADAPTER_SCALE = 0.5
ROPE_BASE = 500000.0
LANES = 128
VMEM_BYTES = 16 * 1024 * 1024
LOAD_BYTES = 52 * 1024 * 1024
PACK_BYTES = 60 * 1024 * 1024


def rotation_factors(positions, head_dim):
    half_dim = head_dim // 2
    inv_freq = jnp.exp(
        -jnp.arange(half_dim, dtype=jnp.float32) * (2.0 / head_dim) * math.log(ROPE_BASE)
    )
    angles = positions.astype(jnp.float32)[:, None] * inv_freq[None, :]
    return jnp.cos(angles), jnp.sin(angles)


ORDER = (((2, 1), (3, 0)), ((1, 2), (3, 0)), ((1, 0), (2, 3)), ((0, 3), (1, 2)))
PLANES = [
    sum(ORDER[a][c][i] << (4 * a + 2 * i) for a in range(4) for i in range(2)) for c in range(2)
]
INDEX = sum(i << (4 * a + ORDER[a][c][i]) for a in range(4) for c in range(2) for i in range(2))


def position():
    column = lax.axis_index("tensor")
    return lax.axis_index("adapter"), column % 2, column // 2


def plane_of(place, core, index):
    both = jnp.where(core == 0, PLANES[0], PLANES[1])
    return (both >> (4 * place + 2 * index)) & 3


def index_of(plane, place):
    return (INDEX >> (4 * plane + place)) & 1


def pack_kernel(ids_in, hidden_in, out_ref, ids_ref, sems):
    requests, width = hidden_in.shape
    half = requests // 2
    ids_copy = pltpu.make_async_copy(ids_in, ids_ref, sems.at[0])
    copies = [
        pltpu.make_async_copy(
            hidden_in.at[pl.ds(i * half, half)],
            out_ref.at[:, pl.ds(i * width, width)],
            sems.at[1 + i],
        )
        for i in range(2)
    ]
    for copy in copies:
        copy.start()
    ids_copy.start()
    ids_copy.wait()
    row = lax.broadcasted_iota(jnp.int32, (half, LANES), 0)
    lane = lax.broadcasted_iota(jnp.int32, (half, LANES), 1)
    row += jnp.where(lane < LANES // 2, 0, half)
    ids = jnp.zeros((half, LANES), jnp.int32)
    for r in range(requests):
        ids = jnp.where(row == r, ids_ref[r], ids)
    out_ref[:, 2 * width :] = ids.astype(jnp.float32).astype(jnp.bfloat16)
    for copy in copies:
        copy.wait()


def pack(request_adapter, hidden):
    requests, width = hidden.shape
    return pl.pallas_call(
        pack_kernel,
        out_shape=pltpu.VMEM((requests // 2, 2 * width + LANES), jnp.bfloat16),
        in_specs=[pl.BlockSpec(memory_space=pltpu.HBM)] * 2,
        out_specs=in_vmem(),
        scratch_shapes=[
            pltpu.SMEM(request_adapter.shape, jnp.int32),
            pltpu.SemaphoreType.DMA((3,)),
        ],
        compiler_params=pltpu.CompilerParams(vmem_limit_bytes=PACK_BYTES),
        name="pack",
    )(request_adapter, hidden)


def down_kernel(*refs):
    *message_refs, down_ref, out_ref, ids_ref, rows_ref = refs
    place = position()[0]
    held, rank, width = down_ref.shape
    half = message_refs[0].shape[0]
    lane = lax.broadcasted_iota(jnp.int32, (half, LANES), 1)
    for k, message_ref in zip((0, 3, 2, 1), message_refs):
        pair = message_ref[:, 2 * width :].astype(jnp.float32)
        swapped = pltpu.roll(pair, LANES // 2, 1)
        for i in range(2):
            start = pl.multiple_of((place ^ k) * 2 * half + i * half, half)
            rows_ref[pl.ds(start, half), :] = message_ref[:, i * width : (i + 1) * width]
            ids_ref[pl.ds(start, half), :] = jnp.where((lane < LANES // 2) == (i == 0), pair, swapped)
    ids = ids_ref[...]
    slot = jnp.transpose(ids)[0:1] - (place * held).astype(jnp.float32)
    product = lax.dot_general(
        down_ref[...].reshape(held * rank, width),
        rows_ref[...],
        (((1,), (1,)), ((), ())),
        preferred_element_type=jnp.float32,
    )
    total = jnp.zeros(out_ref.shape, jnp.float32)
    for s in range(held):
        total += jnp.where(slot == s, product[s * rank : (s + 1) * rank], 0.0)
    out_ref[...] = total


def up_kernel(ids_ref, *refs):
    shrink_refs, query_refs, kv_refs = refs[:4], refs[4:6], refs[6:8]
    *out_refs, rows_ref, terms_ref = refs[8:]
    place, core, side = position()
    shrink = shrink_refs[0][...].astype(jnp.float32)
    for ref in shrink_refs[1:]:
        shrink += ref[...].astype(jnp.float32)
    rank = shrink.shape[0] // 3
    every = shrink.shape[1]
    shrink = jnp.concatenate([shrink, jnp.zeros((LANES - 3 * rank, every), jnp.float32)], axis=0)
    rows_ref[...] = jnp.transpose(shrink)
    rows = every // 2
    block = out_refs[0].shape[0]
    starts = [pl.multiple_of(plane_of(place, core, i) * block, block) for i in range(2)]
    shrink = jnp.concatenate([rows_ref[pl.ds(start, block), :] for start in starts], axis=0)
    ids = jnp.concatenate([ids_ref[pl.ds(start, block), :] for start in starts], axis=0)
    lane = lax.broadcasted_iota(jnp.int32, (rows, LANES), 1)
    count = query_refs[0].shape[0]

    each = LANES // rank
    here = [ids - c * each == (lane // rank).astype(jnp.float32) for c in range(count // each)]

    def spread(part):
        part = jnp.concatenate([part] * each, axis=1)
        return jnp.concatenate(
            [jnp.where(mask, part, 0.0).astype(jnp.bfloat16) for mask in here], axis=1
        )

    query, key, value = [spread(shrink[:, i * rank : (i + 1) * rank]) for i in range(3)]
    width = query_refs[0].shape[2]
    half = kv_refs[0].shape[3]

    def product(rows_spread, factors):
        return ADAPTER_SCALE * jnp.dot(
            rows_spread,
            factors.reshape(count * rank, factors.shape[-1]),
            preferred_element_type=jnp.float32,
        )

    keys, new_values = [], []
    for which in range(2):
        column = pl.multiple_of((core ^ which) * width, width)
        terms_ref[:, pl.ds(column, width)] = product(query, query_refs[which][...])
        keys.append(product(key, kv_refs[which][:, 0]))
        new_values.append(product(value, kv_refs[which][:, 1]))
    for i, parts in enumerate((keys, new_values)):
        both = jnp.concatenate(parts, axis=1)
        both = jnp.where(core == 0, both, pltpu.roll(both, half, 1))
        terms_ref[:, 2 * width + i * LANES : 2 * width + (i + 1) * LANES] = both
    terms = terms_ref[...]
    largest = jnp.max(jnp.abs(terms), axis=1, keepdims=True)
    power = jnp.clip(jnp.ceil(jnp.log2(jnp.maximum(largest, 1e-30))), -100.0, 100.0)
    terms_ref[...] = terms * jnp.exp2(-power)
    total = terms.shape[1]
    for k, out_ref in enumerate(out_refs):
        at = pl.multiple_of((side ^ k) * block, block)
        out_ref[:, :total] = terms_ref[pl.ds(at, block), :]
        out_ref[:, total:] = jnp.broadcast_to(
            jnp.where((side ^ k) == 0, power[:block], power[block:]), (block, LANES)
        )


def attend_kernel(message, *refs):
    (
        term_ref,
        base_query_ref,
        base_key_ref,
        base_value_ref,
        lengths_ref,
        cosine_ref,
        sine_ref,
        keys_ref,
        values_ref,
    ) = refs[:9]
    (
        out_ref,
        fresh_key_ref,
        fresh_value_ref,
        mixed_ref,
        fresh_ref,
        query_ref,
        score_ref,
        weight_ref,
        new_weight_ref,
        sems,
    ) = refs[-10:]
    place, core, side = position()
    g = index_of(2 * side + core, place) ^ message
    requests = base_query_ref.shape[0]
    slots, head = keys_ref.shape[2], keys_ref.shape[3]
    wide = base_query_ref.shape[1] // keys_ref.shape[1]
    group = wide // head
    half = head // 2
    total = term_ref.shape[1] - LANES
    scale = jnp.exp2(term_ref[:, total : total + 1])
    cosine, sine = cosine_ref[...], sine_ref[...]
    cosine = jnp.concatenate([cosine, cosine], axis=1)
    sine = jnp.concatenate([-sine, sine], axis=1)

    def rotate(u):
        return (u * cosine + pltpu.roll(u, half, 1) * sine).astype(jnp.bfloat16)

    def columns(width):
        return pl.ds(pl.multiple_of(g * width, width), width)

    base = base_query_ref[:, columns(wide)].astype(jnp.float32)
    for h in range(group):
        c = h * head
        u = base[:, c : c + head] + term_ref[:, c : c + head] * scale
        query_ref[pl.ds(h, requests, stride=group), :] = rotate(u).astype(jnp.float32)
    u = base_key_ref[:, columns(head)].astype(jnp.float32)
    new_key = rotate(u + term_ref[:, wide : wide + head] * scale)
    u = base_value_ref[:, columns(head)].astype(jnp.float32)
    new_value = (u + term_ref[:, wide + head : wide + 2 * head] * scale).astype(jnp.bfloat16)
    fresh_ref[0] = new_key
    fresh_ref[1] = new_value
    fresh_copies = [
        pltpu.make_async_copy(fresh_ref.at[i], ref.at[:, columns(head)], sems.at[i])
        for i, ref in enumerate((fresh_key_ref, fresh_value_ref))
    ]
    for copy in fresh_copies:
        copy.start()
    new_key, new_value = new_key.astype(jnp.float32), new_value.astype(jnp.float32)

    inv_sqrt = 1.0 / math.sqrt(head)
    zero = jnp.zeros((group, head), jnp.float32)

    def four(ref, r):
        parts = [ref[(r + i) * group : (r + i + 1) * group, :] for i in range(4)]
        return jnp.concatenate(
            [
                jnp.concatenate([parts[i], zero] if i % 2 == 0 else [zero, parts[i]], axis=1)
                for i in range(4)
            ],
            axis=0,
        ).astype(jnp.bfloat16)

    for r in range(0, requests, 4):
        keys = [keys_ref[r + i, g] for i in range(4)]
        keys = jnp.concatenate(
            [jnp.concatenate(keys[:2], axis=1), jnp.concatenate(keys[2:], axis=1)], axis=0
        )
        scores = lax.dot_general(
            four(query_ref, r), keys, (((1,), (1,)), ((), ())), preferred_element_type=jnp.float32
        )
        for i in range(4):
            score_ref[(r + i) * group : (r + i + 1) * group, :] = scores[
                i * group : (i + 1) * group, (i // 2) * slots : (i // 2 + 1) * slots
            ]
    row = lax.broadcasted_iota(jnp.int32, (requests, requests), 0)
    lane = lax.broadcasted_iota(jnp.int32, (requests, requests), 1)
    limits = jnp.where(row == lane, lengths_ref[...].astype(jnp.float32), 0.0)
    limits = jnp.broadcast_to(jnp.sum(limits, axis=1, keepdims=True), (requests, slots))
    slot = lax.broadcasted_iota(jnp.int32, (group, slots), 1).astype(jnp.float32)
    for r in range(requests):
        rows = slice(r * group, (r + 1) * group)
        new_score = (
            jnp.sum(query_ref[rows, :] * new_key[r : r + 1], axis=1, keepdims=True) * inv_sqrt
        )
        scores = jnp.where(slot < limits[r : r + 1], score_ref[rows, :] * inv_sqrt, -jnp.inf)
        row_max = jnp.maximum(jnp.max(scores, axis=1, keepdims=True), new_score)
        weights = jnp.exp(scores - row_max)
        new_weight = jnp.exp(new_score - row_max)
        total = jnp.sum(weights, axis=1, keepdims=True) + new_weight
        weight_ref[rows, :] = weights / total
        new_weight_ref[rows, :] = jnp.broadcast_to(new_weight / total, (group, head))
    for r in range(0, requests, 4):
        values = [values_ref[r + i, g] for i in range(4)]
        values = jnp.concatenate(
            [jnp.concatenate([values[i], values[i + 2]], axis=1) for i in range(2)], axis=0
        )
        mixed = jnp.dot(four(weight_ref, r), values, preferred_element_type=jnp.float32)
        for i in range(4):
            rows = slice((r + i) * group, (r + i + 1) * group)
            new_weight = new_weight_ref[rows, :].astype(jnp.bfloat16).astype(jnp.float32)
            score_ref[rows, :] = (
                mixed[i * group : (i + 1) * group, (i // 2) * head : (i // 2 + 1) * head]
                + new_weight * new_value[r + i : r + i + 1]
            )
    for h in range(group):
        mixed_ref[:, h * head : (h + 1) * head] = score_ref[
            pl.ds(h, requests, stride=group), :
        ].astype(jnp.bfloat16)
    copy = pltpu.make_async_copy(mixed_ref, out_ref.at[:, columns(wide)], sems.at[2])
    copy.start()
    for fresh_copy in fresh_copies:
        fresh_copy.wait()
    copy.wait()


def attend(message, arrays, before):
    base_queries, base_keys, base_values = arrays[1:4]
    requests, head = base_queries.shape[0], arrays[-1].shape[3]
    kv_heads = arrays[-1].shape[1]
    wide = base_queries.shape[1] // kv_heads
    rows = requests * wide // head
    shapes = [
        jax.ShapeDtypeStruct(a.shape, a.dtype) for a in (base_queries, base_keys, base_values)
    ]
    in_hbm = pl.BlockSpec(memory_space=pltpu.HBM)
    return pl.pallas_call(
        functools.partial(attend_kernel, message),
        out_shape=shapes,
        in_specs=[in_vmem()] * len(arrays) + [in_hbm] * len(before),
        out_specs=[in_hbm] * 3,
        input_output_aliases={len(arrays) + i: i for i in range(len(before))},
        scratch_shapes=[
            pltpu.VMEM((requests, wide), jnp.bfloat16),
            pltpu.VMEM((2, requests, head), jnp.bfloat16),
            pltpu.VMEM((rows, head), jnp.float32),
            pltpu.VMEM((rows, head), jnp.float32),
            pltpu.VMEM((rows, head), jnp.float32),
            pltpu.VMEM((rows, head), jnp.float32),
            pltpu.SemaphoreType.DMA((3,)),
        ],
        compiler_params=pltpu.CompilerParams(vmem_limit_bytes=VMEM_BYTES),
        name="attend",
    )(*arrays, *before)


def load_kernel(*refs):
    count = (len(refs) - 1) // 2
    sems = refs[-1]
    copies = [
        pltpu.make_async_copy(refs[i], refs[count + i], sems.at[i]) for i in range(count)
    ]
    for copy in copies:
        copy.start()
    for copy in copies:
        copy.wait()


def load(arrays):
    return pl.pallas_call(
        load_kernel,
        out_shape=[pltpu.VMEM(a.shape, a.dtype) for a in arrays],
        in_specs=[pl.BlockSpec(memory_space=pltpu.HBM)] * len(arrays),
        out_specs=[in_vmem()] * len(arrays),
        scratch_shapes=[pltpu.SemaphoreType.DMA((len(arrays),))],
        compiler_params=pltpu.CompilerParams(vmem_limit_bytes=LOAD_BYTES),
        cost_estimate=pl.CostEstimate(
            flops=0, bytes_accessed=sum(a.size for a in arrays) * 4, transcendentals=0
        ),
        name="load",
    )(*arrays)


def in_vmem():
    return pl.BlockSpec(memory_space=pltpu.VMEM)


def call(kernel, name, out_shape, scratch, arrays):
    return pl.pallas_call(
        kernel,
        out_shape=out_shape,
        in_specs=[in_vmem()] * len(arrays),
        out_specs=[in_vmem()] * len(out_shape),
        scratch_shapes=scratch,
        compiler_params=pltpu.CompilerParams(vmem_limit_bytes=VMEM_BYTES),
        name=name,
    )(*arrays)


def step(value, axis, size, k):
    return lax.ppermute(value, axis, [(i, i ^ k) for i in range(size)])


def exchange(value, axis, size):
    return [value] + [step(value, axis, size, k) for k in range(size - 1, 0, -1)]


def few_body(
    hidden,
    base_queries,
    base_keys,
    base_values,
    adapter_down_weight,
    adapter_up_query,
    adapter_up_key_value,
    cached_keys,
    cached_values,
    request_adapter,
    lengths,
):
    planes, columns = lax.axis_size("adapter"), lax.axis_size("tensor")
    requests = hidden.shape[0]
    every = requests * planes
    rank3 = adapter_down_weight.shape[1]
    head = cached_keys.shape[3]
    kv_heads = cached_keys.shape[1]
    heads = base_queries.shape[1] // head

    f32, bf16 = jnp.float32, jnp.bfloat16
    message = pack(request_adapter, hidden)
    mirror = step(message, "adapter", planes, planes - 1)
    near = step(message, "adapter", planes, 1)
    everyone = [message, mirror, step(mirror, "adapter", planes, 1), near]
    sent = [
        [
            (a * columns + t, ORDER[a][t % 2][(t // 2) ^ k] * columns + a)
            for a in range(planes)
            for t in range(columns)
        ]
        for k in range(2)
    ]
    message, early_query = lax.optimization_barrier((message, adapter_up_query))
    everyone[0] = message
    other_query = step(early_query, "tensor", columns, 1)
    other_key_value = step(adapter_up_key_value, "tensor", columns, 1)
    (
        adapter_down_weight,
        adapter_up_query,
        adapter_up_key_value,
        base_queries,
        base_keys,
        base_values,
        cached_keys,
        cached_values,
    ) = load(
        [
            adapter_down_weight,
            adapter_up_query,
            adapter_up_key_value,
            base_queries,
            base_keys,
            base_values,
            cached_keys,
            cached_values,
        ]
    )
    partial, every_id = call(
        down_kernel,
        "down",
        [jax.ShapeDtypeStruct((rank3, every), f32), jax.ShapeDtypeStruct((every, LANES), f32)],
        [pltpu.VMEM((every, hidden.shape[1]), bf16)],
        [*everyone, adapter_down_weight],
    )
    summed = functools.reduce(jnp.add, exchange(partial, "tensor", columns)).astype(bf16)
    shrink = exchange(summed, "adapter", planes)
    width = 2 * adapter_up_query.shape[2] + 4 * adapter_up_key_value.shape[3]
    terms = call(
        up_kernel,
        "up",
        [jax.ShapeDtypeStruct((requests, width + LANES), f32)] * 2,
        [pltpu.VMEM((every, LANES), f32), pltpu.VMEM((every // 2, width), f32)],
        [
            every_id,
            *shrink,
            adapter_up_query,
            other_query,
            adapter_up_key_value,
            other_key_value,
        ],
    )
    arrived = [
        lax.ppermute(term.astype(jnp.float16), ("adapter", "tensor"), sent[k]).astype(f32)
        for k, term in enumerate(terms)
    ]
    cosine, sine = rotation_factors(lengths, head)
    outs = []
    for k, term in enumerate(arrived):
        arrays = [
            term,
            base_queries,
            base_keys,
            base_values,
            lengths[None, :],
            cosine,
            sine,
            cached_keys,
            cached_values,
        ]
        outs = attend(k, arrays, outs)
    return tuple(outs)


def rotate_pairs(vectors, positions):
    half_dim = vectors.shape[-1] // 2
    inv_freq = jnp.exp(
        -jnp.arange(half_dim, dtype=jnp.float32) * (2.0 / vectors.shape[-1]) * math.log(ROPE_BASE)
    )
    angles = positions.astype(jnp.float32)[:, None, None] * inv_freq[None, None, :]
    cosine = jnp.cos(angles)
    sine_part = jnp.sin(angles)
    front_half = vectors[..., :half_dim]
    back_half = vectors[..., half_dim:]
    return jnp.concatenate(
        [front_half * cosine - back_half * sine_part, front_half * sine_part + back_half * cosine],
        axis=-1,
    )


def attend_cache(query_vector, key_new, value_new, cached_keys, cached_values, lengths):
    local_requests, query_heads, head_dim = query_vector.shape
    kv_heads = key_new.shape[1]
    grouped = query_vector.reshape(local_requests, kv_heads, query_heads // kv_heads, head_dim)
    inv_sqrt = 1.0 / math.sqrt(head_dim)
    cache_scores = (
        jnp.einsum("rkge,rkpe->rkgp", grouped, cached_keys, preferred_element_type=jnp.float32)
        * inv_sqrt
    )
    in_cache = jnp.arange(cached_keys.shape[2], dtype=jnp.int32)[None, :] < lengths[:, None]
    cache_scores = jnp.where(in_cache[:, None, None, :], cache_scores, -jnp.inf)
    new_score = (
        jnp.einsum("rkge,rke->rkg", grouped, key_new, preferred_element_type=jnp.float32) * inv_sqrt
    )
    row_max = jnp.maximum(jnp.max(cache_scores, axis=-1), new_score)
    cache_weights = jnp.exp(cache_scores - row_max[..., None])
    new_weight = jnp.exp(new_score - row_max)
    softmax_sum = jnp.sum(cache_weights, axis=-1) + new_weight
    cache_weights = (cache_weights / softmax_sum[..., None]).astype(jnp.bfloat16)
    new_weight = (new_weight / softmax_sum).astype(jnp.bfloat16)
    mixed = jnp.einsum(
        "rkgp,rkpe->rkge", cache_weights, cached_values, preferred_element_type=jnp.float32
    )
    mixed = (
        mixed
        + new_weight.astype(jnp.float32)[..., None] * value_new.astype(jnp.float32)[:, :, None, :]
    )
    return mixed.reshape(local_requests, query_heads * head_dim).astype(jnp.bfloat16)


def many_body(
    hidden,
    base_queries,
    base_keys,
    base_values,
    adapter_down_weight,
    adapter_up_query,
    adapter_up_key_value,
    cached_keys,
    cached_values,
    request_adapter,
    lengths,
):
    owner_index = lax.axis_index("adapter")
    owning_requests = lax.axis_size("adapter")
    holding_count = adapter_down_weight.shape[0]
    rank_width = adapter_up_query.shape[1]
    local_requests = hidden.shape[0]
    everyone, every_id = (
        lax.all_gather(hidden, "adapter", axis=0, tiled=True),
        lax.all_gather(request_adapter, "adapter", axis=0, tiled=True),
    )
    every_row = everyone.shape[0]
    slot_of = every_id - owner_index * holding_count
    picked = slot_of[:, None] == jnp.arange(holding_count, dtype=jnp.int32)[None, :]
    picked_float = picked.astype(jnp.float32)
    flattened_lowered = adapter_down_weight.reshape(
        holding_count * 3 * rank_width, adapter_down_weight.shape[2]
    )
    partial_value = lax.dot_general(
        everyone, flattened_lowered, (((1,), (1,)), ((), ())), preferred_element_type=jnp.float32
    )
    summed = lax.psum(partial_value, "tensor")
    mine = jnp.sum(
        summed.reshape(every_row, holding_count, 3 * rank_width) * picked_float[:, :, None], axis=1
    )
    shrink_rank = lax.psum(mine.astype(jnp.bfloat16), "adapter").astype(jnp.float32)
    shrink_rank = shrink_rank.astype(jnp.bfloat16)

    def expand_rank(segment, factors):
        rows_used = jnp.take(factors, every_id, axis=0)
        rank_product = jnp.einsum(
            "rj,rjc->rc", segment, rows_used, preferred_element_type=jnp.float32
        )
        column_width = rank_product.shape[1]
        return (ADAPTER_SCALE * rank_product).reshape(
            owning_requests, every_row // owning_requests, 1, column_width
        )

    query_portion = expand_rank(shrink_rank[:, :rank_width], adapter_up_query)
    key_portion = expand_rank(
        shrink_rank[:, rank_width : 2 * rank_width], adapter_up_key_value[:, 0]
    )
    value_portion = expand_rank(shrink_rank[:, 2 * rank_width :], adapter_up_key_value[:, 1])
    arrived = (
        lax.all_to_all(
            lax.all_to_all(query_portion, "adapter", split_axis=0, concat_axis=2, tiled=True),
            "tensor",
            split_axis=2,
            concat_axis=0,
            tiled=True,
        ),
        lax.all_to_all(
            lax.all_to_all(key_portion, "adapter", split_axis=0, concat_axis=2, tiled=True),
            "tensor",
            split_axis=2,
            concat_axis=0,
            tiled=True,
        ),
        lax.all_to_all(
            lax.all_to_all(value_portion, "adapter", split_axis=0, concat_axis=2, tiled=True),
            "tensor",
            split_axis=2,
            concat_axis=0,
            tiled=True,
        ),
    )

    def columns(values):
        return jnp.transpose(values, (1, 2, 0, 3)).reshape(local_requests, -1)

    query_update = columns(arrived[0])
    key_update = columns(arrived[1])
    value_update = columns(arrived[2])
    head_dim = cached_keys.shape[3]
    kv_heads = cached_keys.shape[1]
    query_heads = base_queries.shape[1] // head_dim
    query_vector = rotate_pairs(
        (base_queries.astype(jnp.float32) + query_update).reshape(
            local_requests, query_heads, head_dim
        ),
        lengths,
    ).astype(jnp.bfloat16)
    fresh_keys = rotate_pairs(
        (base_keys.astype(jnp.float32) + key_update).reshape(local_requests, kv_heads, head_dim),
        lengths,
    ).astype(jnp.bfloat16)
    fresh_values = (base_values.astype(jnp.float32) + value_update).astype(jnp.bfloat16)
    attention = attend_cache(
        query_vector,
        fresh_keys,
        fresh_values.reshape(local_requests, kv_heads, head_dim),
        cached_keys,
        cached_values,
        lengths,
    )
    return (attention, fresh_keys.reshape(local_requests, kv_heads * head_dim), fresh_values)


def solution(mesh):
    few = mesh.shape["adapter"] == 4 and mesh.shape["tensor"] == 4
    return jax.shard_map(
        few_body if few else many_body,
        mesh=mesh,
        in_specs=(
            P(("groups", "adapter"), "tensor"),
            P(("groups", "adapter"), "tensor"),
            P(("groups", "adapter"), "tensor"),
            P(("groups", "adapter"), "tensor"),
            P("adapter", None, "tensor"),
            P(None, None, ("adapter", "tensor")),
            P(None, None, None, ("adapter", "tensor")),
            P(("groups", "adapter"), "tensor", None, None),
            P(("groups", "adapter"), "tensor", None, None),
            P(("groups", "adapter")),
            P(("groups", "adapter")),
        ),
        out_specs=(
            P(("groups", "adapter"), "tensor"),
            P(("groups", "adapter"), "tensor"),
            P(("groups", "adapter"), "tensor"),
        ),
        check_vma=False,
    )
```
